256 devices in a mesh: view: 32 (over x, z), head: 8 (over y, core).
Axes of the slice: x: 4, y: 4, z: 8, core: 2. Of those that a mesh axis runs over, the one named last changes fastest.
Arguments:
- features: bfloat16 [65536, 1024], P(('view', 'head')), may hold values from -6 to 6
- attend_weight: bfloat16 [2, 3, 1024, 1024], P(None, None, 'view', 'head'), may hold values from -0.1875 to 0.1875
- output_weight: bfloat16 [2, 1024, 1024], P(None, 'view'), may hold values from -0.1875 to 0.1875
- fast_init: bfloat16 [2, 16, 3, 64, 512], P(None, 'head', None, None, 'view'), may hold values from -0.75 to 0.75
- update_mask: int32 [32, 2048], P('view'), may hold values 0 or 1
Outputs:
- refined: bfloat16 [65536, 1024], P(('view', 'head'))
The draws below stay inside these ranges and needn't reach their ends.
All inputs are finite; a program needn't handle non-finite values. No bound on the sum of `update_mask` on one device may be relied on, other than what follows from the above.
Results may differ from the reference program's by a relative error of at most 0.035.
Values may be sent and summed in bfloat16 or wider, within the bound.
A program may use at most 64 MiB of HBM per device.

```python
import jax
import jax.numpy as jnp
from jax import lax

D = 1024
H = 16
DH = 64
FH = 512
VIEW_LEN = 2048
BLOCKS = 2
NS_STEPS = 5
VIEWS = 32
TOKENS = 65536


def plant(drawn, own_key, least, largest):
    extent = drawn.shape
    place = [jax.random.randint(jax.random.fold_in(own_key, axis), (), 0, extent[axis]) for axis in range(len(extent))]
    drawn = drawn.at[tuple(place)].set(least)
    longest = extent.index(max(extent))
    place[longest] = (place[longest] + 1) % extent[longest]
    return drawn.at[tuple(place)].set(largest)


def levels(stream_key, shape, shards, least, high):
    loudness, own = 1.0, jax.random.fold_in(stream_key, 6)
    for position, blocks in shards:
        draws = jnp.exp(jax.random.uniform(jax.random.fold_in(own, position), (blocks,), jnp.float32, least / len(shards), high / len(shards)))
        loudness = loudness * jnp.repeat(draws, shape[position] // blocks).reshape([-1 if axis == position else 1 for axis in range(len(shape))])
    return loudness


def gaussian(rng, shape, deviation, bound, pieces=(), dtype=jnp.bfloat16):
    result = deviation * jax.random.normal(rng, shape, jnp.float32)
    if pieces:
        result = result * levels(rng, shape, pieces, -0.22, 0.18)
    return jnp.clip(result, -bound, bound).astype(dtype)


def setup_inputs(seed: int = 0) -> dict:
    splits = jax.random.split(jax.random.key(seed), 6)
    features = gaussian(splits[0], (TOKENS, D), 1.0, 6.0, ((0, 256),))
    attend_weight = gaussian(splits[1], (BLOCKS, 3, D, D), D ** -0.5, 0.1875, ((2, 32), (3, 8)))
    output_weight = gaussian(splits[2], (BLOCKS, D, D), D ** -0.5, 0.1875, ((1, 32),))
    fast_init = gaussian(splits[3], (BLOCKS, H, 3, DH, FH), DH ** -0.5, 0.75, ((1, 8), (4, 32)))
    update_mask = plant((jax.random.randint(splits[4], (VIEWS, VIEW_LEN), 0, 4) < 3).astype(jnp.int32), jax.random.fold_in(splits[4], 1), 0, 1)
    return dict(features=features, attend_weight=attend_weight, output_weight=output_weight, fast_init=fast_init, update_mask=update_mask)


newton_coeffs = (3.4445, -4.775, 2.0315)
learn_rate = 1.0
score_scale = 0.25

def normalize(values, epsilon):
    return values * lax.rsqrt(lax.optimization_barrier(jnp.mean(values * values, axis=-1, keepdims=True)) + epsilon)

def newton_step(current, gram_matrix):
    squared = jnp.einsum('...de,...ef->...df', gram_matrix, gram_matrix, precision=lax.Precision.HIGHEST)
    polynomial = newton_coeffs[1] * gram_matrix + newton_coeffs[2] * squared
    return newton_coeffs[0] * current + jnp.einsum('...de,...ef->...df', polynomial, current, precision=lax.Precision.HIGHEST)

def orthogonalize(gradients):
    squares = lax.optimization_barrier(jnp.sum(gradients * gradients, axis=(-2, -1), keepdims=True))
    current = gradients * lax.rsqrt(squares + 1e-06)
    for _ in range(NS_STEPS):
        gram_matrix = jnp.einsum('...df,...ef->...de', current, current, precision=lax.Precision.HIGHEST)
        current = newton_step(current, gram_matrix)
    return current

def fast_gradient(keys, values, mask, weights):
    wide = weights.astype(jnp.float32)
    key_wide = keys.astype(jnp.float32)
    first = jnp.einsum('thd,hdf->thf', key_wide, wide[:, 0])
    third = jnp.einsum('thd,hdf->thf', key_wide, wide[:, 1])
    sigma = jax.nn.sigmoid(first)
    hidden = (first * sigma * third).astype(jnp.bfloat16)
    target = (-(mask[:, None, None].astype(jnp.float32) * values.astype(jnp.float32))).astype(jnp.bfloat16)
    back = jnp.einsum('thd,hdf->thf', target.astype(jnp.float32), wide[:, 2])
    d_third = (back * first * sigma).astype(jnp.bfloat16)
    d_first = (back * third * sigma * (1.0 + first * (1.0 - sigma))).astype(jnp.bfloat16)
    grad_first = jnp.einsum('thd,thf->hdf', key_wide, d_first.astype(jnp.float32))
    grad_third = jnp.einsum('thd,thf->hdf', key_wide, d_third.astype(jnp.float32))
    grad_last = jnp.einsum('thd,thf->hdf', target.astype(jnp.float32), hidden.astype(jnp.float32))
    return jnp.stack([grad_first, grad_third, grad_last], axis=1)

def fast_apply(queries, weights):
    wide = weights.astype(jnp.float32)
    query_wide = queries.astype(jnp.float32)
    first = jnp.einsum('thd,hdf->thf', query_wide, wide[:, 0])
    third = jnp.einsum('thd,hdf->thf', query_wide, wide[:, 1])
    hidden = (first * jax.nn.sigmoid(first) * third).astype(jnp.bfloat16)
    output = jnp.einsum('thf,hdf->thd', hidden.astype(jnp.float32), wide[:, 2])
    return normalize(output, 1e-05)

def attend(queries, keys, values):
    scores = jnp.einsum('qhd,khd->hqk', queries.astype(jnp.float32), keys.astype(jnp.float32)) * score_scale
    expo = jnp.exp(scores)
    probs = (expo / lax.optimization_barrier(jnp.sum(expo, axis=-1, keepdims=True))).astype(jnp.bfloat16)
    return jnp.einsum('hqk,khd->qhd', probs.astype(jnp.float32), values.astype(jnp.float32))

def reference(features, attend_weight, output_weight, fast_init, update_mask):
    stream = features
    for layer in range(BLOCKS):
        normed = normalize(stream.astype(jnp.float32), 1e-05).astype(jnp.bfloat16)
        packed = jnp.stack([jnp.dot(normed, attend_weight[layer, which], preferred_element_type=jnp.float32) for which in range(3)], axis=1).astype(jnp.bfloat16)
        packed = packed.reshape(VIEWS, VIEW_LEN, 3, H, DH)
        queries = normalize(packed[:, :, 0].astype(jnp.float32), 1e-05).astype(jnp.bfloat16)
        keys = normalize(packed[:, :, 1].astype(jnp.float32), 1e-05).astype(jnp.bfloat16)
        values = packed[:, :, 2]
        initial = fast_init[layer]

        def accumulate(total, inputs):
            return (total + fast_gradient(inputs[0], inputs[1], inputs[2], initial), None)
        gradients, _ = lax.scan(accumulate, jnp.zeros((H, 3, DH, FH), jnp.float32), (keys, values, update_mask))
        updated = (initial.astype(jnp.float32) - learn_rate * orthogonalize(gradients)).astype(jnp.bfloat16)

        def mix_view(inputs):
            return (attend(inputs[0], inputs[1], inputs[2]) + fast_apply(inputs[0], updated)).astype(jnp.bfloat16)
        mixed = lax.map(mix_view, (queries, keys, values)).reshape(TOKENS, D)
        projected = jnp.dot(mixed, output_weight[layer], preferred_element_type=jnp.float32)
        stream = (stream.astype(jnp.float32) + projected).astype(jnp.bfloat16)
    return stream
```

```python
import functools
import math

import jax
import jax.numpy as jnp
from jax import lax
from jax.experimental import pallas as pl
from jax.experimental.pallas import tpu as pltpu
from jax.sharding import PartitionSpec as P

BLOCKS = 2
NS_STEPS = 5
NEWTON = (3.4445, -4.775, 2.0315)
LEARN_RATE = 1.0
SCORE_SCALE = 0.25
EPS = 1e-05

NX, NZ, NY = 4, 8, 4
NV, NH = NX * NZ, 2 * NY

F32 = jnp.float32
BF16 = jnp.bfloat16
NT = (((1,), (1,)), ((), ()))
TN = (((0,), (0,)), ((), ()))


def dot(a, b, dims=(((1,), (0,)), ((), ())), precision=None):
    return lax.dot_general(a, b, dims, precision=precision, preferred_element_type=F32)


def low_lanes(shape):
    return lax.broadcasted_iota(jnp.int32, shape, len(shape) - 1) < 64


def head_norm(x):
    low = low_lanes(x.shape)
    sq = x * x
    first = jnp.sum(jnp.where(low, sq, 0.0), axis=-1, keepdims=True)
    second = jnp.sum(jnp.where(low, 0.0, sq), axis=-1, keepdims=True)
    return lax.rsqrt(jnp.where(low, first, second) * (1.0 / 64) + EPS)


def sigmoid(x):
    return 0.5 + 0.5 * jnp.tanh(0.5 * x)


def gray(p):
    return p + (p // 2) * (1 - 2 * (p % 2))


def start_copy(src, dst, send, recv, view, head):
    pltpu.make_async_remote_copy(
        src_ref=src,
        dst_ref=dst,
        send_sem=send,
        recv_sem=recv,
        device_id=(view, head),
        device_id_type=pl.DeviceIdType.MESH,
    ).start()


def wait_bytes(ref, sem):
    pltpu.make_async_copy(ref, ref, sem).wait()


def kernel(
    features,
    attend,
    fast,
    outw,
    mask,
    result,
    stream,
    gathered,
    qkv_w,
    fast_w,
    out_w,
    queries,
    scaled,
    keys,
    values,
    wide,
    total,
    to_sum,
    parts,
    summed,
    attended,
    to_mix,
    mixed,
    wz_recv,
    wx_recv,
    w_send,
    o_recv,
    o_send,
    og_recv,
    og_send,
    g_recv,
    g_send,
    r_recv,
    r_send,
    m_recv,
    m_send,
):
    view, head = lax.axis_index("view"), lax.axis_index("head")
    x, z = view // NZ, view % NZ
    y, core = head // 2, head % 2
    tokens = stream.shape[0]
    length = tokens * NH
    sib = y * 2 + (1 - core)
    right = ((y + 1) % NY) * 2 + core
    left = ((y + NY - 1) % NY) * 2 + core
    opposite = ((y + 2) % NY) * 2 + core
    half = tokens // 2

    def aligned(value, to):
        return pl.multiple_of(value, to)

    stream[...] = features[...]
    for b in range(BLOCKS):
        for j in range(3):
            qkv_w[b, pl.ds(aligned(view * 32, 32), 32), j * 128 : (j + 1) * 128] = attend[b, j]
        fast_w[b, :, pl.ds(aligned(view * 16, 16), 16), :] = fast[b]

    barrier = pltpu.get_barrier_semaphore()

    def greet_view(d, carry):
        pl.semaphore_signal(
            barrier, inc=1, device_id=((view + d) % NV, head), device_id_type=pl.DeviceIdType.MESH
        )
        return carry

    def greet_head(d, carry):
        pl.semaphore_signal(
            barrier, inc=1, device_id=(view, (head + d) % NH), device_id_type=pl.DeviceIdType.MESH
        )
        return carry

    lax.fori_loop(1, NV, greet_view, 0)
    lax.fori_loop(1, NH, greet_head, 0)
    pl.semaphore_wait(barrier, NV - 1 + NH - 1)

    def weights_z(b):
        own = qkv_w.at[b, pl.ds(aligned(view * 32, 32), 32)]
        own_fast = fast_w.at[b, :, pl.ds(aligned(view * 16, 16), 16)]

        def send(d, carry):
            to = x * NZ + (z + d) % NZ
            start_copy(own, own, w_send.at[b, 0], wz_recv.at[b, 0], to, head)
            return carry

        def send_fast(d, carry):
            to = x * NZ + (z + d) % NZ
            start_copy(own_fast, own_fast, w_send.at[b, 1], wz_recv.at[b, 1], to, head)
            return carry

        lax.fori_loop(1, NZ, send, 0)
        lax.fori_loop(1, NZ, send_fast, 0)

    def weights_x(b):
        wait_bytes(qkv_w.at[b, pl.ds(0, 32 * (NZ - 1))], wz_recv.at[b, 0])
        own = qkv_w.at[b, pl.ds(aligned(x * 256, 256), 256)]
        for d in (1, 3, 2):
            to = ((x + d) % NX) * NZ + z
            start_copy(own, own, w_send.at[b, 0], wx_recv.at[b, 0], to, head)
        wait_bytes(fast_w.at[b, :, pl.ds(0, 16 * (NZ - 1))], wz_recv.at[b, 1])
        own_fast = fast_w.at[b, :, pl.ds(aligned(x * 128, 128), 128)]
        for d in (1, 3, 2):
            to = ((x + d) % NX) * NZ + z
            start_copy(own_fast, own_fast, w_send.at[b, 1], wx_recv.at[b, 1], to, head)

    group = view // 4

    def output_fetch():
        rows = pl.ds(aligned(view * 32, 32), 32)
        target_group = (group - head + NH) % NH

        def send(i, carry):
            to = target_group * 4 + i

            @pl.when(to == view)
            def _():
                pltpu.make_async_copy(outw, out_w.at[:, rows], o_recv).start()

            @pl.when(to != view)
            def _():
                start_copy(outw, out_w.at[:, rows], o_send, o_recv, to, head)

            return carry

        lax.fori_loop(0, 4, send, 0)

    def output_rows(of_head):
        return pl.ds(aligned(((group + of_head) % NH) * 128, 128), 128)

    def output_share(b):
        own = out_w.at[b, output_rows(head)]
        for to in (right, left, opposite):
            start_copy(own, own, og_send.at[b], og_recv.at[b, 0], view, to)
        start_copy(own, own, og_send.at[b], og_recv.at[b, 1], view, sib)

    def output_forward(b):
        wait_bytes(out_w.at[b, pl.ds(0, 3 * 128)], og_recv.at[b, 0])
        for of_head in (right, left, opposite):
            piece = out_w.at[b, output_rows(of_head)]
            start_copy(piece, piece, og_send.at[b], og_recv.at[b, 1], view, sib)

    weights_z(0)

    def block(b, carry):
        def tokens_of(of_head, part=None):
            if part is None:
                return gathered.at[b, pl.ds(aligned(of_head * tokens, tokens), tokens)]
            return gathered.at[b, pl.ds(aligned(of_head * tokens + part * half, half), half)]

        def send_tokens(of_head, part, recv, to):
            piece = tokens_of(of_head, part)
            start_copy(piece, piece, g_send.at[b], g_recv.at[b, recv], view, to)

        for part in range(2):
            wide_rows = stream[part * half : (part + 1) * half, :].astype(F32)
            inv = lax.rsqrt(jnp.mean(wide_rows * wide_rows, axis=-1, keepdims=True) + EPS)
            gathered[b, pl.ds(aligned(head * tokens + part * half, half), half), :] = (
                wide_rows * inv
            ).astype(BF16)
        send_tokens(head, None, 6, sib)
        send_tokens(head, 0, 0, right)
        send_tokens(head, 1, 3, left)
        send_tokens(head, 1, 1, right)
        send_tokens(head, 0, 2, left)

        @pl.when(b == 0)
        def _():
            weights_z(1)
            weights_x(0)
            output_fetch()

        total[...] = jnp.zeros_like(total)
        wait_bytes(qkv_w.at[b, pl.ds(0, 256 * (NX - 1))], wx_recv.at[b, 0])
        wait_bytes(fast_w.at[b, :, pl.ds(0, 128 * (NX - 1))], wx_recv.at[b, 1])
        for j in range(3):
            weights = fast_w[b, j]
            low = low_lanes(weights.shape)
            wide[j, 0:512, :] = jnp.where(low, weights, jnp.zeros_like(weights))
            wide[j, 512:1024, :] = jnp.where(low, jnp.zeros_like(weights), weights)

        def chunk(s, carry):
            @pl.when(s == 1)
            def _():
                wait_bytes(tokens_of(sib), g_recv.at[b, 6])

            @pl.when(s == 2)
            def _():
                wait_bytes(tokens_of(left, 0), g_recv.at[b, 0])
                send_tokens(left, 0, 4, right)
                wait_bytes(tokens_of(right, 1), g_recv.at[b, 3])
                send_tokens(right, 1, 5, left)
                wait_bytes(tokens_of(right, 0), g_recv.at[b, 2])
                send_tokens(right, None, 7, sib)
                wait_bytes(tokens_of(left, 1), g_recv.at[b, 1])
                send_tokens(left, None, 8, sib)

            @pl.when(s == 3)
            def _():
                wait_bytes(tokens_of(((y + 1) % NY) * 2 + 1 - core), g_recv.at[b, 7])

            @pl.when(s == 5)
            def _():
                wait_bytes(tokens_of(((y + 3) % NY) * 2 + 1 - core), g_recv.at[b, 8])

            @pl.when(s == 6)
            def _():
                wait_bytes(tokens_of(opposite, 0), g_recv.at[b, 4])
                wait_bytes(tokens_of(opposite, 1), g_recv.at[b, 5])
                send_tokens(opposite, None, 9, sib)

            @pl.when(s == 7)
            def _():
                wait_bytes(tokens_of(((y + 2) % NY) * 2 + 1 - core), g_recv.at[b, 9])

            @pl.when(jnp.logical_and(b == 0, s == 4))
            def _():
                weights_x(1)

            source = ((y + gray(s // 2)) % NY) * 2 + (core + s % 2) % 2
            rows = pl.ds(aligned(source * tokens, tokens), tokens)
            packed = dot(gathered[b, rows, :], qkv_w[b]).astype(BF16)
            q = packed[:, 0:128].astype(F32)
            k = packed[:, 128:256].astype(F32)
            v = packed[:, 256:384]
            low = low_lanes((tokens, 128))
            q = q * head_norm(q)
            queries[rows, :] = q.astype(BF16)
            scaled[rows, :] = (q * (SCORE_SCALE * math.log2(math.e))).astype(BF16)
            k = (k * head_norm(k)).astype(BF16)
            keys[rows, :] = k
            one = jnp.ones_like(v)
            values[0, rows, :] = jnp.where(low, v, one)
            values[1, rows, :] = jnp.where(low, one, v)
            sign = -mask[:, rows].astype(F32)
            zero = jnp.zeros_like(v)
            for h in range(2):
                kh = jnp.where(low, k, zero) if h == 0 else jnp.where(low, zero, k)
                vh = jnp.where(low, v, zero) if h == 0 else jnp.where(low, zero, v)
                for part in range(2):
                    f = slice(h * 512 + part * 256, h * 512 + part * 256 + 256)
                    first = dot(wide[0, f, :], k, NT)
                    third = dot(wide[1, f, :], k, NT)
                    back = dot(wide[2, f, :], v, NT) * sign
                    sigma = sigmoid(first)
                    silu = first * sigma
                    hidden = (silu * third * sign).astype(BF16)
                    d_third = (back * silu).astype(BF16)
                    d_first = (back * third * (sigma + silu * (1.0 - sigma))).astype(BF16)
                    to = slice(part * 256, part * 256 + 256)
                    total[0, to, :] += dot(d_first, kh)
                    total[1, to, :] += dot(d_third, kh)
                    total[2, to, :] += dot(hidden, vh)
            return carry

        lax.fori_loop(0, NH, chunk, 0)

        for j in range(3):
            to_sum[j * 512 : (j + 1) * 512, :] = total[j].astype(BF16)

        def scatter(d, carry):
            to = (view + d) % NV
            start_copy(
                to_sum.at[pl.ds(aligned(to * 48, 16), 48)],
                parts.at[b, NV - 1 - d],
                r_send.at[b, 0],
                r_recv.at[b, 0],
                to,
                head,
            )
            return carry

        lax.fori_loop(1, NV, scatter, 0)

        @pl.when(b == 0)
        def _():
            wait_bytes(out_w.at[:, pl.ds(0, 128)], o_recv)

        output_share(b)

        def reduce_parts():
            wait_bytes(parts.at[b], r_recv.at[b, 0])
            mine = pl.ds(aligned(view * 48, 16), 48)

            def add(d, value):
                return value + parts[b, d].astype(F32)

            value = lax.fori_loop(0, NV - 1, add, to_sum[mine, :].astype(F32))
            summed[b, mine, :] = value.astype(BF16)

            def spread(d, carry):
                to = (view + d) % NV
                piece = summed.at[b, mine]
                start_copy(piece, piece, r_send.at[b, 1], r_recv.at[b, 1], to, head)
                return carry

            lax.fori_loop(1, NV, spread, 0)

        def attend_rows(i, carry):
            @pl.when(i == 4)
            def _():
                reduce_parts()

            rows = pl.ds(aligned(i * 256, 256), 256)
            q = scaled[rows, :]
            low = low_lanes(q.shape)
            zero = jnp.zeros_like(q)
            out = []
            for h in range(2):
                qh = jnp.where(low, q, zero) if h == 0 else jnp.where(low, zero, q)
                weighted = jnp.zeros((256, 128), F32)
                for part in range(4):
                    at = slice(part * length // 4, (part + 1) * length // 4)
                    expo = jnp.exp2(dot(qh, keys[at, :], NT)).astype(BF16)
                    weighted = weighted + dot(expo, values[h, at, :])
                out.append(weighted / pltpu.roll(weighted, 64, 1))
            attended[rows, :] = jnp.where(low_lanes(out[0].shape), out[0], out[1])
            return carry

        lax.fori_loop(0, length // 256, attend_rows, 0)
        output_forward(b)

        wait_bytes(summed.at[b, pl.ds(0, 48 * (NV - 1))], r_recv.at[b, 1])
        row = lax.broadcasted_iota(jnp.int32, (128, 128), 0)
        col = lax.broadcasted_iota(jnp.int32, (128, 128), 1)
        same = (row < 64) == (col < 64)
        eye = row == col
        exact = functools.partial(dot, precision=lax.Precision.HIGHEST)
        grams, scales = [], []
        for j in range(3):
            gradient = summed[b, j * 512 : (j + 1) * 512, :]
            gram = jnp.where(same, dot(gradient, gradient, TN), 0.0)
            diagonal = jnp.where(eye, gram, 0.0)
            squares = jnp.sum(jnp.where(same, jnp.sum(diagonal, axis=1, keepdims=True), 0.0), axis=0, keepdims=True)
            scale = lax.rsqrt(squares + 1e-06)
            scales.append(scale)
            grams.append(gram * (scale * scale))
        chains = [None] * 3
        for step in range(NS_STEPS):
            for j in range(3):
                gram = grams[j]
                poly = (
                    jnp.where(eye, NEWTON[0], 0.0)
                    + NEWTON[1] * gram
                    + NEWTON[2] * exact(gram, gram)
                )
                chains[j] = poly if step == 0 else exact(poly, chains[j])
                if step < NS_STEPS - 1:
                    grams[j] = exact(exact(poly, gram), poly)
        for j in range(3):
            gradient = summed[b, j * 512 : (j + 1) * 512, :]
            upper = chains[j].astype(BF16)
            lower = (chains[j] - upper.astype(F32)).astype(BF16)
            current = (dot(gradient, upper) + dot(gradient, lower)) * scales[j]
            updated = (fast_w[b, j].astype(F32) - LEARN_RATE * current).astype(BF16)
            low = low_lanes(updated.shape)
            wide[j, 0:512, :] = jnp.where(low, updated, jnp.zeros_like(updated))
            wide[j, 512:1024, :] = jnp.where(low, jnp.zeros_like(updated), updated)

        def apply_rows(s, carry):
            to = ((y + gray(3 - s // 2)) % NY) * 2 + (core + 1 - s % 2) % 2
            rows = pl.ds(aligned(to * tokens, tokens), tokens)
            q = queries[rows, :]
            applied = jnp.zeros((tokens, 128), F32)
            for part in range(4):
                f = slice(part * 256, part * 256 + 256)
                first = dot(q, wide[0, f, :], NT)
                third = dot(q, wide[1, f, :], NT)
                hidden = (first * sigmoid(first) * third).astype(BF16)
                applied = applied + dot(hidden, wide[2, f, :])
            to_mix[rows, :] = (attended[rows, :] + applied * head_norm(applied)).astype(BF16)
            columns = pl.ds(aligned(head * 128, 128), 128)

            @pl.when(s < NH - 1)
            def _():
                start_copy(
                    to_mix.at[rows], mixed.at[b, :, columns], m_send.at[b], m_recv.at[b], view, to
                )

            @pl.when(s == NH - 1)
            def _():
                mixed[b, :, columns] = to_mix[rows, :]

            return carry

        lax.fori_loop(0, NH, apply_rows, 0)

        wait_bytes(out_w.at[b, pl.ds(0, 4 * 128)], og_recv.at[b, 1])
        wait_bytes(mixed.at[b, :, pl.ds(0, 128 * (NH - 1))], m_recv.at[b])
        for part in range(4):
            n = slice(part * 256, part * 256 + 256)
            projected = dot(mixed[b], out_w[b, :, n])
            stream[:, n] = (stream[:, n].astype(F32) + projected).astype(BF16)

        wait_bytes(to_mix.at[pl.ds(0, tokens * (NH - 1))], m_send.at[b])
        wait_bytes(to_sum.at[pl.ds(0, 48 * (NV - 1))], r_send.at[b, 0])
        wait_bytes(summed.at[b, pl.ds(0, 48 * (NV - 1))], r_send.at[b, 1])
        wait_bytes(gathered.at[b, pl.ds(0, tokens * 7)], g_send.at[b])
        wait_bytes(out_w.at[b, pl.ds(0, 128 * 7)], og_send.at[b])
        return carry

    lax.fori_loop(0, BLOCKS, block, 0)
    result[...] = stream[...]

    for b in range(BLOCKS):
        wait_bytes(qkv_w.at[b, pl.ds(0, 32 * (NZ - 1) + 256 * (NX - 1))], w_send.at[b, 0])
        wait_bytes(fast_w.at[b, :, pl.ds(0, 16 * (NZ - 1) + 128 * (NX - 1))], w_send.at[b, 1])

    @pl.when(head == 0)
    def _():
        wait_bytes(out_w.at[:, pl.ds(0, 96)], o_send)

    @pl.when(head != 0)
    def _():
        wait_bytes(out_w.at[:, pl.ds(0, 128)], o_send)


def shards(features, attend_weight, output_weight, fast_init, update_mask):
    tokens, width = features.shape
    length = tokens * NH
    pieces = jnp.transpose(fast_init, (0, 2, 4, 1, 3)).reshape(BLOCKS, 3, 16, 128)
    vmem = pl.BlockSpec(memory_space=pltpu.VMEM)
    dma = pltpu.SemaphoreType.DMA
    return pl.pallas_call(
        kernel,
        out_shape=jax.ShapeDtypeStruct((tokens, width), BF16),
        in_specs=[vmem] * 5,
        out_specs=vmem,
        scratch_shapes=[
            pltpu.VMEM((tokens, width), BF16),
            pltpu.VMEM((BLOCKS, length, width), BF16),
            pltpu.VMEM((BLOCKS, width, 384), BF16),
            pltpu.VMEM((BLOCKS, 3, 512, 128), BF16),
            pltpu.VMEM((BLOCKS, width, width), BF16),
            pltpu.VMEM((length, 128), BF16),
            pltpu.VMEM((length, 128), BF16),
            pltpu.VMEM((length, 128), BF16),
            pltpu.VMEM((2, length, 128), BF16),
            pltpu.VMEM((3, 1024, 128), BF16),
            pltpu.VMEM((3, 512, 128), F32),
            pltpu.VMEM((1536, 128), BF16),
            pltpu.VMEM((BLOCKS, NV - 1, 48, 128), BF16),
            pltpu.VMEM((BLOCKS, 1536, 128), BF16),
            pltpu.VMEM((length, 128), F32),
            pltpu.VMEM((length, 128), BF16),
            pltpu.VMEM((BLOCKS, tokens, width), BF16),
            dma((BLOCKS, 2)),
            dma((BLOCKS, 2)),
            dma((BLOCKS, 2)),
            dma,
            dma,
            dma((BLOCKS, 2)),
            dma((BLOCKS,)),
            dma((BLOCKS, 10)),
            dma((BLOCKS,)),
            dma((BLOCKS, 2)),
            dma((BLOCKS, 2)),
            dma((BLOCKS,)),
            dma((BLOCKS,)),
        ],
        compiler_params=pltpu.CompilerParams(
            collective_id=0, has_side_effects=True, vmem_limit_bytes=56 * 1024 * 1024
        ),
        name="lact",
    )(features, attend_weight, pieces, output_weight, update_mask)


def solution(mesh):
    return jax.shard_map(
        shards,
        mesh=mesh,
        in_specs=(
            P(("view", "head"), None),
            P(None, None, "view", "head"),
            P(None, "view", None),
            P(None, "head", None, None, "view"),
            P("view", None),
        ),
        out_specs=P(("view", "head"), None),
        check_vma=False,
    )
```

```python
import math

import jax
import jax.numpy as jnp
from jax import lax
from jax.experimental import pallas as pl
from jax.experimental.pallas import tpu as pltpu
from jax.sharding import PartitionSpec as P

BLOCKS = 2
NS_STEPS = 5
NEWTON = (3.4445, -4.775, 2.0315)
LEARN_RATE = 1.0
SCORE_SCALE = 0.25
EPS = 1e-05

NX, NZ, NY = 4, 8, 4
NV, NH = NX * NZ, 2 * NY

F32 = jnp.float32
BF16 = jnp.bfloat16
NT = (((1,), (1,)), ((), ()))
TN = (((0,), (0,)), ((), ()))


def dot(a, b, dims=(((1,), (0,)), ((), ())), precision=None):
    return lax.dot_general(a, b, dims, precision=precision, preferred_element_type=F32)


def low_lanes(shape):
    return lax.broadcasted_iota(jnp.int32, shape, len(shape) - 1) < 64


def head_norm(x):
    low = low_lanes(x.shape)
    sq = x * x
    first = jnp.sum(jnp.where(low, sq, 0.0), axis=-1, keepdims=True)
    second = jnp.sum(jnp.where(low, 0.0, sq), axis=-1, keepdims=True)
    return lax.rsqrt(jnp.where(low, first, second) * (1.0 / 64) + EPS)


def split(x):
    upper = x.astype(BF16)
    return upper, (x - upper.astype(F32)).astype(BF16)


def head_norm_wide(x):
    upper, lower = split(x * x)
    row = lax.broadcasted_iota(jnp.int32, (x.shape[1], x.shape[1]), 0) // 64
    col = lax.broadcasted_iota(jnp.int32, (x.shape[1], x.shape[1]), 1) // 64
    ones = jnp.where(row == col, 1.0, 0.0).astype(BF16)
    return lax.rsqrt((dot(upper, ones) + dot(lower, ones)) * (1.0 / 64) + EPS)


def exact(a, b):
    return dot(a, b, precision=lax.Precision.HIGHEST)


def triple(a, b):
    a_upper, a_lower = split(a)
    b_upper, b_lower = split(b)
    return dot(a_upper, b_upper) + (dot(a_upper, b_lower) + dot(a_lower, b_upper))


def sigmoid(x):
    return 0.5 + 0.5 * jnp.tanh(0.5 * x)


def gray(p):
    return p + (p // 2) * (1 - 2 * (p % 2))


def start_copy(src, dst, send, recv, view, head):
    pltpu.make_async_remote_copy(
        src_ref=src,
        dst_ref=dst,
        send_sem=send,
        recv_sem=recv,
        device_id=(view, head),
        device_id_type=pl.DeviceIdType.MESH,
    ).start()


def wait_bytes(ref, sem):
    pltpu.make_async_copy(ref, ref, sem).wait()


def kernel(
    features,
    attend,
    fast,
    outw,
    mask,
    result,
    stream,
    gathered,
    qkv_w,
    fast_w,
    out_w,
    queries,
    scaled,
    keys,
    values,
    wide,
    total,
    to_sum,
    parts,
    summed,
    attended,
    to_mix,
    mixed,
    w_recv,
    w_send,
    o_recv,
    o_send,
    og_recv,
    og_send,
    g_recv,
    g_send,
    r_recv,
    r_send,
    m_recv,
    m_send,
):
    view, head = lax.axis_index("view"), lax.axis_index("head")
    x, z = view // NZ, view % NZ
    y, core = head // 2, head % 2
    tokens = stream.shape[0]
    length = tokens * NH
    sib = y * 2 + (1 - core)
    right = ((y + 1) % NY) * 2 + core
    left = ((y + NY - 1) % NY) * 2 + core
    opposite = ((y + 2) % NY) * 2 + core
    half = tokens // 2
    pair = tokens * 2

    def aligned(value, to):
        return pl.multiple_of(value, to)

    def normalize(b, part):
        rows = slice(part * half, (part + 1) * half)
        wide_rows = stream[rows, :].astype(F32)
        inv = lax.rsqrt(jnp.mean(wide_rows * wide_rows, axis=-1, keepdims=True) + EPS)
        gathered[b, pl.ds(aligned(head * tokens + part * half, half), half), :] = (
            wide_rows * inv
        ).astype(BF16)

    barrier = pltpu.get_barrier_semaphore()

    def greet(to_view, to_head):
        pl.semaphore_signal(
            barrier, inc=1, device_id=(to_view, to_head), device_id_type=pl.DeviceIdType.MESH
        )

    def greet_z(d, carry):
        greet(x * NZ + (z + d) % NZ, head)
        return carry

    for to in (right, left, sib):
        greet(view, to)
    lax.fori_loop(1, NZ, greet_z, 0)
    for d in range(1, NX):
        greet(((x + d) % NX) * NZ + z, head)
    stream[...] = features[...]
    for b in range(BLOCKS):
        for j in range(3):
            qkv_w[b, pl.ds(aligned(view * 32, 32), 32), j * 128 : (j + 1) * 128] = attend[b, j]
            fast_w[b, j, x, z] = fast[b, j]
    normalize(0, 0)
    normalize(0, 1)
    pl.semaphore_wait(barrier, 3 + NZ - 1 + NX - 1)

    def tokens_of(b, of_head, part=None):
        if part is None:
            return gathered.at[b, pl.ds(aligned(of_head * tokens, tokens), tokens)]
        return gathered.at[b, pl.ds(aligned(of_head * tokens + part * half, half), half)]

    def send_tokens(b, of_head, part, recv, to):
        piece = tokens_of(b, of_head, part)
        start_copy(piece, piece, g_send.at[b], g_recv.at[b, recv], view, to)

    def launch_tokens(b, part):
        send_tokens(b, head, part, 6, sib)
        if part == 0:
            send_tokens(b, head, 0, 0, right)
        else:
            send_tokens(b, head, 1, 3, left)
            send_tokens(b, head, 1, 1, right)
            send_tokens(b, head, 0, 2, left)

    def projections_z(b):
        own = qkv_w.at[b, pl.ds(aligned(view * 32, 32), 32)]

        def send(d, carry):
            to = x * NZ + (z + d) % NZ
            start_copy(own, own, w_send.at[b, 0], w_recv.at[b, 0], to, head)
            return carry

        lax.fori_loop(1, NZ, send, 0)

    def projections_x(b):
        wait_bytes(qkv_w.at[b, pl.ds(0, 32 * (NZ - 1))], w_recv.at[b, 0])
        own = qkv_w.at[b, pl.ds(aligned(x * 256, 256), 256)]
        for d in (1, 3, 2):
            to = ((x + d) % NX) * NZ + z
            start_copy(own, own, w_send.at[b, 1], w_recv.at[b, 1], to, head)

    def fast_x(b):
        own = fast_w.at[b, :, x, z]
        for d in (1, 3, 2):
            to = ((x + d) % NX) * NZ + z
            start_copy(own, own, w_send.at[b, 2], w_recv.at[b, 2], to, head)

    def fast_z(b):
        wait_bytes(fast_w.at[b, :, pl.ds(0, NX - 1), 0], w_recv.at[b, 2])
        own = fast_w.at[b, :, :, z]

        def send(d, carry):
            to = x * NZ + (z + d) % NZ
            start_copy(own, own, w_send.at[b, 3], w_recv.at[b, 3], to, head)
            return carry

        lax.fori_loop(1, NZ, send, 0)

    group = view // 4

    def output_fetch():
        rows = pl.ds(aligned(view * 32, 32), 32)
        target_group = (group - head + NH) % NH

        def send(i, carry):
            to = target_group * 4 + i

            @pl.when(to == view)
            def _():
                pltpu.make_async_copy(outw, out_w.at[:, rows], o_recv).start()

            @pl.when(to != view)
            def _():
                start_copy(outw, out_w.at[:, rows], o_send, o_recv, to, head)

            return carry

        lax.fori_loop(0, 4, send, 0)

    def output_rows(of_head):
        return pl.ds(aligned(((group + of_head) % NH) * 128, 128), 128)

    def output_share(b):
        own = out_w.at[b, output_rows(head)]
        for to in (right, left, opposite):
            start_copy(own, own, og_send.at[b], og_recv.at[b, 0], view, to)
        start_copy(own, own, og_send.at[b], og_recv.at[b, 1], view, sib)

    def output_forward(b):
        wait_bytes(out_w.at[b, pl.ds(0, 3 * 128)], og_recv.at[b, 0])
        for of_head in (right, left, opposite):
            piece = out_w.at[b, output_rows(of_head)]
            start_copy(piece, piece, og_send.at[b], og_recv.at[b, 1], view, sib)

    projections_z(0)
    launch_tokens(0, 0)
    launch_tokens(0, 1)
    fast_x(0)
    projections_x(0)
    fast_z(0)
    projections_z(1)
    fast_x(1)

    def block(b, carry):
        def project(s):
            @pl.when(s == 0)
            def _():
                wait_bytes(tokens_of(b, sib), g_recv.at[b, 6])
                wait_bytes(qkv_w.at[b, pl.ds(0, 256 * (NX - 1))], w_recv.at[b, 1])

                @pl.when(b == 0)
                def _():
                    output_fetch()

            @pl.when(s == 1)
            def _():
                wait_bytes(tokens_of(b, left, 0), g_recv.at[b, 0])
                send_tokens(b, left, 0, 4, right)
                wait_bytes(tokens_of(b, right, 1), g_recv.at[b, 3])
                send_tokens(b, right, 1, 5, left)
                wait_bytes(tokens_of(b, right, 0), g_recv.at[b, 2])
                send_tokens(b, right, None, 7, sib)
                wait_bytes(tokens_of(b, left, 1), g_recv.at[b, 1])
                send_tokens(b, left, None, 8, sib)

                @pl.when(b == 0)
                def _():
                    projections_x(1)
                    fast_z(1)

                wait_bytes(tokens_of(b, sib), g_recv.at[b, 7])

            @pl.when(s == 2)
            def _():
                wait_bytes(tokens_of(b, sib), g_recv.at[b, 8])

            @pl.when(s == 3)
            def _():
                wait_bytes(tokens_of(b, opposite, 0), g_recv.at[b, 4])
                wait_bytes(tokens_of(b, opposite, 1), g_recv.at[b, 5])
                send_tokens(b, opposite, None, 9, sib)
                wait_bytes(tokens_of(b, sib), g_recv.at[b, 9])

            rows = pl.ds(aligned(((y + gray(s)) % NY) * pair, pair), pair)
            packed = dot(gathered[b, rows, :], qkv_w[b]).astype(BF16)
            both = packed[:, 0:256].astype(F32)
            both = both * head_norm_wide(both)
            q = both[:, 0:128]
            v = packed[:, 256:384]
            queries[rows, :] = q.astype(BF16)
            scaled[rows, :] = (q * (SCORE_SCALE * math.log2(math.e))).astype(BF16)
            keys[rows, :] = both[:, 128:256].astype(BF16)
            low = low_lanes(v.shape)
            one = jnp.ones_like(v)
            values[0, rows, :] = jnp.where(low, v, one)
            values[1, rows, :] = jnp.where(low, one, v)

        def differentiate(s):
            @pl.when(s == 0)
            def _():
                wait_bytes(fast_w.at[b, :, :, pl.ds(0, NZ - 1)], w_recv.at[b, 3])
                total[...] = jnp.zeros_like(total)
                for j in range(3):
                    weights = fast_w[b, j].reshape(512, 128)
                    low = low_lanes(weights.shape)
                    wide[j, 0:512, :] = jnp.where(low, weights, jnp.zeros_like(weights))
                    wide[j, 512:1024, :] = jnp.where(low, jnp.zeros_like(weights), weights)

            rows = pl.ds(aligned(((y + gray(s)) % NY) * pair, pair), pair)
            k = keys[rows, :]
            low = low_lanes(k.shape)
            zero = jnp.zeros_like(k)
            sign = -mask[:, rows].astype(F32)
            for h in range(2):
                v = values[h, rows, :]
                kh = jnp.where(low, k, zero) if h == 0 else jnp.where(low, zero, k)
                vh = jnp.where(low, v, zero) if h == 0 else jnp.where(low, zero, v)
                f = slice(h * 512, h * 512 + 512)
                first = dot(wide[0, f, :], k, NT)
                third = dot(wide[1, f, :], k, NT)
                back = dot(wide[2, f, :], v, NT) * sign
                sigma = sigmoid(first)
                silu = first * sigma
                hidden = (silu * third * sign).astype(BF16)
                d_third = (back * silu).astype(BF16)
                d_first = (back * third * (sigma + silu * (1.0 - sigma))).astype(BF16)
                total[0] += dot(d_first, kh)
                total[1] += dot(d_third, kh)
                total[2] += dot(hidden, vh)

        def turn(u, carry):
            s = b * (u // 2) + (1 - b) * (u % 4)
            kind = b * (u % 2) + (1 - b) * (u // 4)

            @pl.when(kind == 0)
            def _():
                project(s)

            @pl.when(kind == 1)
            def _():
                differentiate(s)

            return carry

        lax.fori_loop(0, 2 * NY, turn, 0)

        for j in range(3):
            to_sum[j * 512 : (j + 1) * 512, :] = total[j].astype(BF16)

        def scatter(d, carry):
            to = (view + d) % NV
            start_copy(
                to_sum.at[pl.ds(aligned(to * 48, 16), 48)],
                parts.at[b, NV - 1 - d],
                r_send.at[b, 0],
                r_recv.at[b, 0],
                to,
                head,
            )
            return carry

        lax.fori_loop(1, NV, scatter, 0)

        @pl.when(b == 0)
        def _():
            wait_bytes(out_w.at[:, pl.ds(0, 128)], o_recv)

        output_share(b)

        def reduce_parts():
            wait_bytes(parts.at[b], r_recv.at[b, 0])
            mine = pl.ds(aligned(view * 48, 16), 48)

            value = to_sum[mine, :].astype(F32) + jnp.sum(parts[b].astype(F32), axis=0)
            summed[b, mine, :] = value.astype(BF16)

            def spread(d, carry):
                to = (view + d) % NV
                piece = summed.at[b, mine]
                start_copy(piece, piece, r_send.at[b, 1], r_recv.at[b, 1], to, head)
                return carry

            lax.fori_loop(1, NV, spread, 0)

        def attend_rows(i, carry):
            @pl.when(i == 1)
            def _():
                reduce_parts()

            rows = pl.ds(aligned(i * 1024, 1024), 1024)
            q = scaled[rows, :]
            low = low_lanes(q.shape)
            zero = jnp.zeros_like(q)
            own = [jnp.where(low, q, zero), jnp.where(low, zero, q)]
            weighted = [jnp.zeros(q.shape, F32)] * 2
            for part in range(length // 256):
                at = slice(part * 256, (part + 1) * 256)
                for h in range(2):
                    expo = jnp.exp2(dot(own[h], keys[at, :], NT)).astype(BF16)
                    weighted[h] = weighted[h] + dot(expo, values[h, at, :])
            out = [each / pltpu.roll(each, 64, 1) for each in weighted]
            attended[rows, :] = jnp.where(low_lanes(out[0].shape), out[0], out[1])
            return carry

        lax.fori_loop(0, length // 1024, attend_rows, 0)
        output_forward(b)

        wait_bytes(summed.at[b, pl.ds(0, 48 * (NV - 1))], r_recv.at[b, 1])
        row = lax.broadcasted_iota(jnp.int32, (128, 128), 0)
        col = lax.broadcasted_iota(jnp.int32, (128, 128), 1)
        same = (row < 64) == (col < 64)
        eye = row == col
        grams, scales = [], []
        for j in range(3):
            gradient = summed[b, j * 512 : (j + 1) * 512, :]
            gram = jnp.where(same, dot(gradient, gradient, TN), 0.0)
            diagonal = jnp.where(eye, gram, 0.0)
            squares = jnp.sum(jnp.where(same, jnp.sum(diagonal, axis=1, keepdims=True), 0.0), axis=0, keepdims=True)
            scale = lax.rsqrt(squares + 1e-06)
            scales.append(scale)
            grams.append(gram * (scale * scale))
        for step in range(NS_STEPS):
            product = exact if step < 2 else triple
            polys = [
                jnp.where(eye, NEWTON[0], 0.0)
                + NEWTON[1] * gram
                + NEWTON[2] * product(gram, gram)
                for gram in grams
            ]
            if step < NS_STEPS - 1:
                halves = [product(poly, gram) for poly, gram in zip(polys, grams)]
                grams = [product(each, poly) for each, poly in zip(halves, polys)]
            if step == 0:
                chains = polys
            else:
                chains = [triple(poly, chain) for poly, chain in zip(polys, chains)]
        for j in range(3):
            gradient = summed[b, j * 512 : (j + 1) * 512, :]
            upper, lower = split(chains[j])
            current = (dot(gradient, upper) + dot(gradient, lower)) * scales[j]
            updated = (fast_w[b, j].reshape(512, 128).astype(F32) - LEARN_RATE * current).astype(BF16)
            low = low_lanes(updated.shape)
            wide[j, 0:512, :] = jnp.where(low, updated, jnp.zeros_like(updated))
            wide[j, 512:1024, :] = jnp.where(low, jnp.zeros_like(updated), updated)

        def apply_rows(s, carry):
            chip = (y + gray(NY - 1 - s)) % NY
            rows = pl.ds(aligned(chip * pair, pair), pair)
            q = queries[rows, :]
            applied = jnp.zeros((pair, 128), F32)
            for part in range(4):
                f = slice(part * 256, part * 256 + 256)
                first = dot(q, wide[0, f, :], NT)
                third = dot(q, wide[1, f, :], NT)
                hidden = (first * sigmoid(first) * third).astype(BF16)
                applied = applied + dot(hidden, wide[2, f, :])
            to_mix[rows, :] = (attended[rows, :] + applied * head_norm(applied)).astype(BF16)
            columns = pl.ds(aligned(head * 128, 128), 128)

            def home(to):
                mine = to_mix.at[pl.ds(aligned(to * tokens, tokens), tokens)]
                start_copy(mine, mixed.at[b, :, columns], m_send.at[b], m_recv.at[b], view, to)

            home(chip * 2 + 1 - core)

            @pl.when(s < NY - 1)
            def _():
                home(chip * 2 + core)

            @pl.when(s == NY - 1)
            def _():
                mixed[b, :, columns] = to_mix[pl.ds(aligned(head * tokens, tokens), tokens), :]

            return carry

        lax.fori_loop(0, NY, apply_rows, 0)

        wait_bytes(out_w.at[b, pl.ds(0, 4 * 128)], og_recv.at[b, 1])
        wait_bytes(mixed.at[b, :, pl.ds(0, 128 * (NH - 1))], m_recv.at[b])
        for part in range(2):
            rows = slice(part * half, (part + 1) * half)
            projected = dot(mixed[b, rows, :], out_w[b])
            stream[rows, :] = (stream[rows, :].astype(F32) + projected).astype(BF16)

            @pl.when(b < BLOCKS - 1)
            def _():
                normalize(b + 1, part)
                launch_tokens(b + 1, part)

        wait_bytes(to_mix.at[pl.ds(0, tokens * (NH - 1))], m_send.at[b])
        wait_bytes(to_sum.at[pl.ds(0, 48 * (NV - 1))], r_send.at[b, 0])
        wait_bytes(summed.at[b, pl.ds(0, 48 * (NV - 1))], r_send.at[b, 1])
        wait_bytes(gathered.at[b, pl.ds(0, tokens * 7)], g_send.at[b])
        wait_bytes(out_w.at[b, pl.ds(0, 128 * 7)], og_send.at[b])
        return carry

    lax.fori_loop(0, BLOCKS, block, 0)
    result[...] = stream[...]

    for b in range(BLOCKS):
        wait_bytes(qkv_w.at[b, pl.ds(0, 32 * (NZ - 1))], w_send.at[b, 0])
        wait_bytes(qkv_w.at[b, pl.ds(0, 256 * (NX - 1))], w_send.at[b, 1])
        wait_bytes(fast_w.at[b, :, pl.ds(0, NX - 1), 0], w_send.at[b, 2])
        wait_bytes(fast_w.at[b, :, :, pl.ds(0, NZ - 1)], w_send.at[b, 3])

    @pl.when(head == 0)
    def _():
        wait_bytes(out_w.at[:, pl.ds(0, 96)], o_send)

    @pl.when(head != 0)
    def _():
        wait_bytes(out_w.at[:, pl.ds(0, 128)], o_send)


def shards(features, attend_weight, output_weight, fast_init, update_mask):
    tokens, width = features.shape
    length = tokens * NH
    pieces = jnp.transpose(fast_init, (0, 2, 4, 1, 3)).reshape(BLOCKS, 3, 16, 128)
    vmem = pl.BlockSpec(memory_space=pltpu.VMEM)
    dma = pltpu.SemaphoreType.DMA
    return pl.pallas_call(
        kernel,
        out_shape=jax.ShapeDtypeStruct((tokens, width), BF16),
        in_specs=[vmem] * 5,
        out_specs=vmem,
        scratch_shapes=[
            pltpu.VMEM((tokens, width), BF16),
            pltpu.VMEM((BLOCKS, length, width), BF16),
            pltpu.VMEM((BLOCKS, width, 384), BF16),
            pltpu.VMEM((BLOCKS, 3, NX, NZ, 16, 128), BF16),
            pltpu.VMEM((BLOCKS, width, width), BF16),
            pltpu.VMEM((length, 128), BF16),
            pltpu.VMEM((length, 128), BF16),
            pltpu.VMEM((length, 128), BF16),
            pltpu.VMEM((2, length, 128), BF16),
            pltpu.VMEM((3, 1024, 128), BF16),
            pltpu.VMEM((3, 512, 128), F32),
            pltpu.VMEM((1536, 128), BF16),
            pltpu.VMEM((BLOCKS, NV - 1, 48, 128), BF16),
            pltpu.VMEM((BLOCKS, 1536, 128), BF16),
            pltpu.VMEM((length, 128), F32),
            pltpu.VMEM((length, 128), BF16),
            pltpu.VMEM((BLOCKS, tokens, width), BF16),
            dma((BLOCKS, 4)),
            dma((BLOCKS, 4)),
            dma,
            dma,
            dma((BLOCKS, 2)),
            dma((BLOCKS,)),
            dma((BLOCKS, 10)),
            dma((BLOCKS,)),
            dma((BLOCKS, 2)),
            dma((BLOCKS, 2)),
            dma((BLOCKS,)),
            dma((BLOCKS,)),
        ],
        compiler_params=pltpu.CompilerParams(
            collective_id=0, has_side_effects=True, vmem_limit_bytes=56 * 1024 * 1024
        ),
        name="lact",
    )(features, attend_weight, pieces, output_weight, update_mask)


def solution(mesh):
    return jax.shard_map(
        shards,
        mesh=mesh,
        in_specs=(
            P(("view", "head"), None),
            P(None, None, "view", "head"),
            P(None, "view", None),
            P(None, "head", None, None, "view"),
            P("view", None),
        ),
        out_specs=P(("view", "head"), None),
        check_vma=False,
    )
```

```python
import math

import jax
import jax.numpy as jnp
from jax import lax
from jax.experimental import pallas as pl
from jax.experimental.pallas import tpu as pltpu
from jax.sharding import PartitionSpec as P

BLOCKS = 2
NS_STEPS = 5
NEWTON = (3.4445, -4.775, 2.0315)
LEARN_RATE = 1.0
SCORE_SCALE = 0.25
EPS = 1e-05

NX, NZ, NY = 4, 8, 4
NV, NH = NX * NZ, 2 * NY

COLUMNS = (slice(0, 128), slice(128, 384))

F32 = jnp.float32
BF16 = jnp.bfloat16
NT = (((1,), (1,)), ((), ()))
TN = (((0,), (0,)), ((), ()))


def dot(a, b, dims=(((1,), (0,)), ((), ())), precision=None):
    return lax.dot_general(a, b, dims, precision=precision, preferred_element_type=F32)


def low_lanes(shape):
    return lax.broadcasted_iota(jnp.int32, shape, len(shape) - 1) < 64


def head_norm(x):
    low = low_lanes(x.shape)
    sq = x * x
    first = jnp.sum(jnp.where(low, sq, 0.0), axis=-1, keepdims=True)
    second = jnp.sum(jnp.where(low, 0.0, sq), axis=-1, keepdims=True)
    return lax.rsqrt(jnp.where(low, first, second) * (1.0 / 64) + EPS)


def split(x):
    upper = x.astype(BF16)
    return upper, (x - upper.astype(F32)).astype(BF16)


def head_norm_wide(x):
    upper, lower = split(x * x)
    row = lax.broadcasted_iota(jnp.int32, (x.shape[1], x.shape[1]), 0) // 64
    col = lax.broadcasted_iota(jnp.int32, (x.shape[1], x.shape[1]), 1) // 64
    ones = jnp.where(row == col, 1.0, 0.0).astype(BF16)
    return lax.rsqrt((dot(upper, ones) + dot(lower, ones)) * (1.0 / 64) + EPS)


def exact(a, b):
    return dot(a, b, precision=lax.Precision.HIGHEST)


def triple(a, b):
    a_upper, a_lower = split(a)
    b_upper, b_lower = split(b)
    return dot(a_upper, b_upper) + (dot(a_upper, b_lower) + dot(a_lower, b_upper))


def sigmoid(x):
    return 0.5 + 0.5 * jnp.tanh(0.5 * x)


def gray(p):
    return p + (p // 2) * (1 - 2 * (p % 2))


def start_copy(src, dst, send, recv, view, head):
    pltpu.make_async_remote_copy(
        src_ref=src,
        dst_ref=dst,
        send_sem=send,
        recv_sem=recv,
        device_id=(view, head),
        device_id_type=pl.DeviceIdType.MESH,
    ).start()


def wait_bytes(ref, sem):
    pltpu.make_async_copy(ref, ref, sem).wait()


def kernel(
    features,
    attend,
    fast,
    outw,
    mask,
    result,
    stream,
    gathered,
    qkv_w,
    fast_w,
    out_w,
    queries,
    scaled,
    keys,
    values,
    wide,
    total,
    to_sum,
    parts,
    summed,
    attended,
    to_mix,
    mixed,
    w_recv,
    w_send,
    o_recv,
    o_send,
    og_recv,
    og_send,
    g_recv,
    g_send,
    r_recv,
    r_send,
    m_recv,
    m_send,
):
    view, head = lax.axis_index("view"), lax.axis_index("head")
    x, z = view // NZ, view % NZ
    y, core = head // 2, head % 2
    tokens = stream.shape[0]
    length = tokens * NH
    sib = y * 2 + (1 - core)
    right = ((y + 1) % NY) * 2 + core
    left = ((y + NY - 1) % NY) * 2 + core
    opposite = ((y + 2) % NY) * 2 + core
    half = tokens // 2
    pair = tokens * 2

    def aligned(value, to):
        return pl.multiple_of(value, to)

    def normalize(b, part):
        rows = slice(part * half, (part + 1) * half)
        wide_rows = stream[rows, :].astype(F32)
        inv = lax.rsqrt(jnp.mean(wide_rows * wide_rows, axis=-1, keepdims=True) + EPS)
        gathered[b, pl.ds(aligned(head * tokens + part * half, half), half), :] = (
            wide_rows * inv
        ).astype(BF16)

    barrier = pltpu.get_barrier_semaphore()

    def greet(to_view, to_head):
        pl.semaphore_signal(
            barrier, inc=1, device_id=(to_view, to_head), device_id_type=pl.DeviceIdType.MESH
        )

    def greet_z(d, carry):
        greet(x * NZ + (z + d) % NZ, head)
        return carry

    for to in (right, left, sib):
        greet(view, to)
    lax.fori_loop(1, NZ, greet_z, 0)
    for d in range(1, NX):
        greet(((x + d) % NX) * NZ + z, head)
    stream[...] = features[...]
    for b in range(BLOCKS):
        for j in range(3):
            qkv_w[b, pl.ds(aligned(view * 32, 32), 32), j * 128 : (j + 1) * 128] = attend[b, j]
            fast_w[b, j, x, z] = fast[b, j]
    normalize(0, 0)
    normalize(0, 1)
    pl.semaphore_wait(barrier, 3 + NZ - 1 + NX - 1)

    def tokens_of(b, of_head, part=None):
        if part is None:
            return gathered.at[b, pl.ds(aligned(of_head * tokens, tokens), tokens)]
        return gathered.at[b, pl.ds(aligned(of_head * tokens + part * half, half), half)]

    def send_tokens(b, of_head, part, recv, to, columns=None):
        piece = tokens_of(b, of_head, part)
        if columns is not None:
            piece = piece.at[:, columns]
        start_copy(piece, piece, g_send.at[b], g_recv.at[b, recv], view, to)

    def launch_tokens(b, part):
        send_tokens(b, head, part, part, right)
        send_tokens(b, head, part, 2 + part, left)
        send_tokens(b, head, part, 4, sib)

    def projections_z(b):
        rows = pl.ds(aligned(view * 32, 32), 32)
        for part, columns in enumerate(COLUMNS):
            own = qkv_w.at[b, rows, columns]

            def send(d, carry):
                to = x * NZ + (z + d) % NZ
                start_copy(own, own, w_send.at[b, part], w_recv.at[b, part], to, head)
                return carry

            lax.fori_loop(1, NZ, send, 0)

    def projections_x(b):
        rows = pl.ds(aligned(x * 256, 256), 256)
        for part, columns in enumerate(COLUMNS):
            wait_bytes(qkv_w.at[b, pl.ds(0, 32 * (NZ - 1)), columns], w_recv.at[b, part])
            own = qkv_w.at[b, rows, columns]
            for d in (1, 3, 2):
                to = ((x + d) % NX) * NZ + z
                start_copy(own, own, w_send.at[b, 2 + part], w_recv.at[b, 2 + part], to, head)

    def fast_x(b):
        own = fast_w.at[b, :, x, z]
        for d in (1, 3, 2):
            to = ((x + d) % NX) * NZ + z
            start_copy(own, own, w_send.at[b, 4], w_recv.at[b, 4], to, head)

    def fast_z(b):
        wait_bytes(fast_w.at[b, :, pl.ds(0, NX - 1), 0], w_recv.at[b, 4])
        own = fast_w.at[b, :, :, z]

        def send(d, carry):
            to = x * NZ + (z + d) % NZ
            start_copy(own, own, w_send.at[b, 5], w_recv.at[b, 5], to, head)
            return carry

        lax.fori_loop(1, NZ, send, 0)

    group = view // 4

    def output_fetch():
        rows = pl.ds(aligned(view * 32, 32), 32)
        target_group = (group - head + NH) % NH

        def send(i, carry):
            to = target_group * 4 + i

            @pl.when(to == view)
            def _():
                pltpu.make_async_copy(outw, out_w.at[:, rows], o_recv).start()

            @pl.when(to != view)
            def _():
                start_copy(outw, out_w.at[:, rows], o_send, o_recv, to, head)

            return carry

        lax.fori_loop(0, 4, send, 0)

    def output_rows(of_head):
        return pl.ds(aligned(((group + of_head) % NH) * 128, 128), 128)

    def output_share(b):
        own = out_w.at[b, output_rows(head)]
        for to in (right, left, opposite):
            start_copy(own, own, og_send.at[b], og_recv.at[b, 0], view, to)
        start_copy(own, own, og_send.at[b], og_recv.at[b, 1], view, sib)

    def output_forward(b):
        wait_bytes(out_w.at[b, pl.ds(0, 3 * 128)], og_recv.at[b, 0])
        for of_head in (right, left, opposite):
            piece = out_w.at[b, output_rows(of_head)]
            start_copy(piece, piece, og_send.at[b], og_recv.at[b, 1], view, sib)

    projections_z(0)
    launch_tokens(0, 0)
    launch_tokens(0, 1)
    fast_x(0)
    projections_x(0)
    fast_z(0)

    def block(b, carry):
        def project(s):
            @pl.when(s == 0)
            def _():
                wait_bytes(tokens_of(b, sib), g_recv.at[b, 4])
                for part, columns in enumerate(COLUMNS):
                    wait_bytes(qkv_w.at[b, pl.ds(0, 256 * (NX - 1)), columns], w_recv.at[b, 2 + part])

                @pl.when(b == 0)
                def _():
                    output_fetch()

            @pl.when(s == 1)
            def _():
                for part in range(2):
                    wait_bytes(tokens_of(b, left, part), g_recv.at[b, part])
                    send_tokens(b, left, part, 7 + part, right, slice(0, 512))
                    wait_bytes(tokens_of(b, right, part), g_recv.at[b, 2 + part])
                    send_tokens(b, right, part, 9 + part, left, slice(512, 1024))
                    send_tokens(b, right, part, 5, sib)
                    send_tokens(b, left, part, 6, sib)
                wait_bytes(tokens_of(b, sib), g_recv.at[b, 5])

            @pl.when(s == 2)
            def _():
                wait_bytes(tokens_of(b, sib), g_recv.at[b, 6])

            @pl.when(s == 3)
            def _():
                for part in range(2):
                    wait_bytes(tokens_of(b, opposite, part).at[:, 0:512], g_recv.at[b, 7 + part])
                    wait_bytes(tokens_of(b, opposite, part).at[:, 512:1024], g_recv.at[b, 9 + part])
                    send_tokens(b, opposite, part, 11, sib)
                wait_bytes(tokens_of(b, sib), g_recv.at[b, 11])

            rows = pl.ds(aligned(((y + gray(s)) % NY) * pair, pair), pair)
            packed = dot(gathered[b, rows, :], qkv_w[b]).astype(BF16)
            both = packed[:, 0:256].astype(F32)
            both = both * head_norm_wide(both)
            q = both[:, 0:128]
            v = packed[:, 256:384]
            queries[rows, :] = q.astype(BF16)
            scaled[rows, :] = (q * (SCORE_SCALE * math.log2(math.e))).astype(BF16)
            keys[rows, :] = both[:, 128:256].astype(BF16)
            low = low_lanes(v.shape)
            one = jnp.ones_like(v)
            values[0, rows, :] = jnp.where(low, v, one)
            values[1, rows, :] = jnp.where(low, one, v)

        def differentiate(s):
            @pl.when(s == 0)
            def _():
                wait_bytes(fast_w.at[b, :, :, pl.ds(0, NZ - 1)], w_recv.at[b, 5])

                @pl.when(b == 0)
                def _():
                    projections_z(1)
                    fast_x(1)

                total[...] = jnp.zeros_like(total)
                for j in range(3):
                    weights = fast_w[b, j].reshape(512, 128)
                    low = low_lanes(weights.shape)
                    wide[j, 0:512, :] = jnp.where(low, weights, jnp.zeros_like(weights))
                    wide[j, 512:1024, :] = jnp.where(low, jnp.zeros_like(weights), weights)

            rows = pl.ds(aligned(((y + gray(s)) % NY) * pair, pair), pair)
            k = keys[rows, :]
            low = low_lanes(k.shape)
            zero = jnp.zeros_like(k)
            sign = -mask[:, rows].astype(F32)
            for h in range(2):
                v = values[h, rows, :]
                kh = jnp.where(low, k, zero) if h == 0 else jnp.where(low, zero, k)
                vh = jnp.where(low, v, zero) if h == 0 else jnp.where(low, zero, v)
                f = slice(h * 512, h * 512 + 512)
                first = dot(wide[0, f, :], k, NT)
                third = dot(wide[1, f, :], k, NT)
                back = dot(wide[2, f, :], v, NT) * sign
                sigma = sigmoid(first)
                silu = first * sigma
                hidden = (silu * third * sign).astype(BF16)
                d_third = (back * silu).astype(BF16)
                d_first = (back * third * (sigma + silu * (1.0 - sigma))).astype(BF16)
                total[0] += dot(d_first, kh)
                total[1] += dot(d_third, kh)
                total[2] += dot(hidden, vh)

        def turn(u, carry):
            s = b * (u // 2) + (1 - b) * (u % 4)
            kind = b * (u % 2) + (1 - b) * (u // 4)

            @pl.when(kind == 0)
            def _():
                project(s)

            @pl.when(kind == 1)
            def _():
                differentiate(s)

            return carry

        lax.fori_loop(0, 2 * NY, turn, 0)

        for j in range(3):
            to_sum[j * 512 : (j + 1) * 512, :] = total[j].astype(BF16)

        def scatter(d, carry):
            to = (view + d) % NV
            start_copy(
                to_sum.at[pl.ds(aligned(to * 48, 16), 48)],
                parts.at[b, NV - 1 - d],
                r_send.at[b, 0],
                r_recv.at[b, 0],
                to,
                head,
            )
            return carry

        lax.fori_loop(1, NV, scatter, 0)

        @pl.when(b == 0)
        def _():
            wait_bytes(out_w.at[:, pl.ds(0, 128)], o_recv)

        output_share(b)

        def reduce_parts():
            wait_bytes(parts.at[b], r_recv.at[b, 0])
            mine = pl.ds(aligned(view * 48, 16), 48)

            value = to_sum[mine, :].astype(F32) + jnp.sum(parts[b].astype(F32), axis=0)
            summed[b, mine, :] = value.astype(BF16)

            def spread(d, carry):
                to = (view + d) % NV
                piece = summed.at[b, mine]
                start_copy(piece, piece, r_send.at[b, 1], r_recv.at[b, 1], to, head)
                return carry

            lax.fori_loop(1, NV, spread, 0)

        def attend_rows(i, carry):
            @pl.when(i == 1)
            def _():
                reduce_parts()

            rows = pl.ds(aligned(i * 1024, 1024), 1024)
            q = scaled[rows, :]
            low = low_lanes(q.shape)
            zero = jnp.zeros_like(q)
            own = [jnp.where(low, q, zero), jnp.where(low, zero, q)]
            weighted = [jnp.zeros(q.shape, F32)] * 2
            for part in range(length // 256):
                at = slice(part * 256, (part + 1) * 256)
                for h in range(2):
                    expo = jnp.exp2(dot(own[h], keys[at, :], NT)).astype(BF16)
                    weighted[h] = weighted[h] + dot(expo, values[h, at, :])
            out = [each / pltpu.roll(each, 64, 1) for each in weighted]
            attended[rows, :] = jnp.where(low_lanes(out[0].shape), out[0], out[1])
            return carry

        lax.fori_loop(0, length // 1024, attend_rows, 0)
        output_forward(b)

        wait_bytes(summed.at[b, pl.ds(0, 48 * (NV - 1))], r_recv.at[b, 1])

        @pl.when(b == 0)
        def _():
            projections_x(1)
            fast_z(1)

        row = lax.broadcasted_iota(jnp.int32, (128, 128), 0)
        col = lax.broadcasted_iota(jnp.int32, (128, 128), 1)
        same = (row < 64) == (col < 64)
        eye = row == col
        grams, scales = [], []
        for j in range(3):
            gradient = summed[b, j * 512 : (j + 1) * 512, :]
            gram = jnp.where(same, dot(gradient, gradient, TN), 0.0)
            diagonal = jnp.where(eye, gram, 0.0)
            squares = jnp.sum(jnp.where(same, jnp.sum(diagonal, axis=1, keepdims=True), 0.0), axis=0, keepdims=True)
            scale = lax.rsqrt(squares + 1e-06)
            scales.append(scale)
            grams.append(gram * (scale * scale))
        for step in range(NS_STEPS):
            product = exact if step < 2 else triple
            polys = [
                jnp.where(eye, NEWTON[0], 0.0)
                + NEWTON[1] * gram
                + NEWTON[2] * product(gram, gram)
                for gram in grams
            ]
            if step < NS_STEPS - 1:
                halves = [product(poly, gram) for poly, gram in zip(polys, grams)]
                grams = [product(each, poly) for each, poly in zip(halves, polys)]
            if step == 0:
                chains = polys
            else:
                chains = [triple(poly, chain) for poly, chain in zip(polys, chains)]
        for j in range(3):
            gradient = summed[b, j * 512 : (j + 1) * 512, :]
            upper, lower = split(chains[j])
            current = (dot(gradient, upper) + dot(gradient, lower)) * scales[j]
            updated = (fast_w[b, j].reshape(512, 128).astype(F32) - LEARN_RATE * current).astype(BF16)
            low = low_lanes(updated.shape)
            wide[j, 0:512, :] = jnp.where(low, updated, jnp.zeros_like(updated))
            wide[j, 512:1024, :] = jnp.where(low, jnp.zeros_like(updated), updated)

        def apply_rows(u, carry):
            part, s = u // NY, u % NY
            chip = (y + gray(NY - 1 - s)) % NY
            near = pl.ds(aligned((chip * 2 + core) * tokens + part * half, half), half)
            far = pl.ds(aligned((chip * 2 + 1 - core) * tokens + part * half, half), half)
            q = jnp.concatenate([queries[far, :], queries[near, :]], axis=0)
            applied = jnp.zeros(q.shape, F32)
            for block_f in range(2):
                f = slice(block_f * 512, block_f * 512 + 512)
                first = dot(q, wide[0, f, :], NT)
                third = dot(q, wide[1, f, :], NT)
                hidden = (first * sigmoid(first) * third).astype(BF16)
                applied = applied + dot(hidden, wide[2, f, :])
            applied = applied * head_norm(applied)
            to_mix[far, :] = (attended[far, :] + applied[0:half]).astype(BF16)
            to_mix[near, :] = (attended[near, :] + applied[half:]).astype(BF16)
            target = mixed.at[
                b, pl.ds(aligned(part * half, half), half), pl.ds(aligned(head * 128, 128), 128)
            ]
            sems = m_send.at[b], m_recv.at[b, part]
            start_copy(to_mix.at[far], target, *sems, view, chip * 2 + 1 - core)

            @pl.when(s < NY - 1)
            def _():
                start_copy(to_mix.at[near], target, *sems, view, chip * 2 + core)

            @pl.when(s == NY - 1)
            def _():
                target[...] = to_mix[near, :]

            return carry

        lax.fori_loop(0, 2 * NY, apply_rows, 0)

        wait_bytes(out_w.at[b, pl.ds(0, 4 * 128)], og_recv.at[b, 1])
        for part in range(2):
            rows = slice(part * half, (part + 1) * half)
            wait_bytes(mixed.at[b, rows, pl.ds(0, 128 * (NH - 1))], m_recv.at[b, part])
            projected = dot(mixed[b, rows, :], out_w[b])
            stream[rows, :] = (stream[rows, :].astype(F32) + projected).astype(BF16)

            @pl.when(b < BLOCKS - 1)
            def _():
                normalize(b + 1, part)
                launch_tokens(b + 1, part)

        wait_bytes(to_mix.at[pl.ds(0, tokens * (NH - 1))], m_send.at[b])
        wait_bytes(to_sum.at[pl.ds(0, 48 * (NV - 1))], r_send.at[b, 0])
        wait_bytes(summed.at[b, pl.ds(0, 48 * (NV - 1))], r_send.at[b, 1])
        wait_bytes(gathered.at[b, pl.ds(0, tokens * 7)], g_send.at[b])
        wait_bytes(out_w.at[b, pl.ds(0, 128 * 7)], og_send.at[b])
        return carry

    lax.fori_loop(0, BLOCKS, block, 0)
    result[...] = stream[...]

    for b in range(BLOCKS):
        for part, columns in enumerate(COLUMNS):
            wait_bytes(qkv_w.at[b, pl.ds(0, 32 * (NZ - 1)), columns], w_send.at[b, part])
            wait_bytes(qkv_w.at[b, pl.ds(0, 256 * (NX - 1)), columns], w_send.at[b, 2 + part])
        wait_bytes(fast_w.at[b, :, pl.ds(0, NX - 1), 0], w_send.at[b, 4])
        wait_bytes(fast_w.at[b, :, :, pl.ds(0, NZ - 1)], w_send.at[b, 5])

    @pl.when(head == 0)
    def _():
        wait_bytes(out_w.at[:, pl.ds(0, 96)], o_send)

    @pl.when(head != 0)
    def _():
        wait_bytes(out_w.at[:, pl.ds(0, 128)], o_send)


def shards(features, attend_weight, output_weight, fast_init, update_mask):
    tokens, width = features.shape
    length = tokens * NH
    pieces = jnp.transpose(fast_init, (0, 2, 4, 1, 3)).reshape(BLOCKS, 3, 16, 128)
    vmem = pl.BlockSpec(memory_space=pltpu.VMEM)
    dma = pltpu.SemaphoreType.DMA
    return pl.pallas_call(
        kernel,
        out_shape=jax.ShapeDtypeStruct((tokens, width), BF16),
        in_specs=[vmem] * 5,
        out_specs=vmem,
        scratch_shapes=[
            pltpu.VMEM((tokens, width), BF16),
            pltpu.VMEM((BLOCKS, length, width), BF16),
            pltpu.VMEM((BLOCKS, width, 384), BF16),
            pltpu.VMEM((BLOCKS, 3, NX, NZ, 16, 128), BF16),
            pltpu.VMEM((BLOCKS, width, width), BF16),
            pltpu.VMEM((length, 128), BF16),
            pltpu.VMEM((length, 128), BF16),
            pltpu.VMEM((length, 128), BF16),
            pltpu.VMEM((2, length, 128), BF16),
            pltpu.VMEM((3, 1024, 128), BF16),
            pltpu.VMEM((3, 512, 128), F32),
            pltpu.VMEM((1536, 128), BF16),
            pltpu.VMEM((BLOCKS, NV - 1, 48, 128), BF16),
            pltpu.VMEM((BLOCKS, 1536, 128), BF16),
            pltpu.VMEM((length, 128), F32),
            pltpu.VMEM((length, 128), BF16),
            pltpu.VMEM((BLOCKS, tokens, width), BF16),
            dma((BLOCKS, 6)),
            dma((BLOCKS, 6)),
            dma,
            dma,
            dma((BLOCKS, 2)),
            dma((BLOCKS,)),
            dma((BLOCKS, 12)),
            dma((BLOCKS,)),
            dma((BLOCKS, 2)),
            dma((BLOCKS, 2)),
            dma((BLOCKS, 2)),
            dma((BLOCKS,)),
        ],
        compiler_params=pltpu.CompilerParams(
            collective_id=0, has_side_effects=True, vmem_limit_bytes=56 * 1024 * 1024
        ),
        name="lact",
    )(features, attend_weight, pieces, output_weight, update_mask)


def solution(mesh):
    return jax.shard_map(
        shards,
        mesh=mesh,
        in_specs=(
            P(("view", "head"), None),
            P(None, None, "view", "head"),
            P(None, "view", None),
            P(None, "head", None, None, "view"),
            P("view", None),
        ),
        out_specs=P(("view", "head"), None),
        check_vma=False,
    )
```

```python
import math

import jax
import jax.numpy as jnp
from jax import lax
from jax.experimental import pallas as pl
from jax.experimental.pallas import tpu as pltpu
from jax.sharding import PartitionSpec as P

BLOCKS = 2
NS_STEPS = 5
NEWTON = (3.4445, -4.775, 2.0315)
LEARN_RATE = 1.0
SCORE_SCALE = 0.25
EPS = 1e-05

NX, NZ, NY = 4, 8, 4
NV, NH = NX * NZ, 2 * NY

COLUMNS = (slice(0, 128), slice(128, 384))

F32 = jnp.float32
BF16 = jnp.bfloat16
NT = (((1,), (1,)), ((), ()))
TN = (((0,), (0,)), ((), ()))


def dot(a, b, dims=(((1,), (0,)), ((), ())), precision=None):
    return lax.dot_general(a, b, dims, precision=precision, preferred_element_type=F32)


def low_lanes(shape):
    return lax.broadcasted_iota(jnp.int32, shape, len(shape) - 1) < 64


def head_norm(x):
    low = low_lanes(x.shape)
    sq = x * x
    first = jnp.sum(jnp.where(low, sq, 0.0), axis=-1, keepdims=True)
    second = jnp.sum(jnp.where(low, 0.0, sq), axis=-1, keepdims=True)
    return lax.rsqrt(jnp.where(low, first, second) * (1.0 / 64) + EPS)


def split(x):
    upper = x.astype(BF16)
    return upper, (x - upper.astype(F32)).astype(BF16)


def head_norm_wide(x):
    upper, lower = split(x * x)
    row = lax.broadcasted_iota(jnp.int32, (x.shape[1], x.shape[1]), 0) // 64
    col = lax.broadcasted_iota(jnp.int32, (x.shape[1], x.shape[1]), 1) // 64
    ones = jnp.where(row == col, 1.0, 0.0).astype(BF16)
    return lax.rsqrt((dot(upper, ones) + dot(lower, ones)) * (1.0 / 64) + EPS)


def exact(a, b):
    return dot(a, b, precision=lax.Precision.HIGHEST)


def triple(a, b):
    a_upper, a_lower = split(a)
    b_upper, b_lower = split(b)
    return dot(a_upper, b_upper) + (dot(a_upper, b_lower) + dot(a_lower, b_upper))


def sigmoid(x):
    return 0.5 + 0.5 * jnp.tanh(0.5 * x)


def gray(p):
    return p + (p // 2) * (1 - 2 * (p % 2))


def start_copy(src, dst, send, recv, view, head):
    pltpu.make_async_remote_copy(
        src_ref=src,
        dst_ref=dst,
        send_sem=send,
        recv_sem=recv,
        device_id=(view, head),
        device_id_type=pl.DeviceIdType.MESH,
    ).start()


def wait_bytes(ref, sem):
    pltpu.make_async_copy(ref, ref, sem).wait()


def kernel(
    features,
    attend,
    fast,
    outw,
    mask,
    result,
    stream,
    gathered,
    qkv_w,
    fast_w,
    out_w,
    queries,
    scaled,
    keys,
    values,
    wide,
    total,
    to_sum,
    a_x,
    c_z,
    a_z,
    c_x,
    middle,
    summed,
    attended,
    to_mix,
    mixed,
    w_recv,
    w_send,
    o_recv,
    o_send,
    og_recv,
    og_send,
    g_recv,
    g_send,
    r_recv,
    r_send,
    m_recv,
    m_send,
):
    view, head = lax.axis_index("view"), lax.axis_index("head")
    x, z = view // NZ, view % NZ
    y, core = head // 2, head % 2
    tokens = stream.shape[0]
    length = tokens * NH
    sib = y * 2 + (1 - core)
    right = ((y + 1) % NY) * 2 + core
    left = ((y + NY - 1) % NY) * 2 + core
    opposite = ((y + 2) % NY) * 2 + core
    half = tokens // 2
    pair = tokens * 2

    def aligned(value, to):
        return pl.multiple_of(value, to)

    def normalize(b, part):
        rows = slice(part * half, (part + 1) * half)
        wide_rows = stream[rows, :].astype(F32)
        inv = lax.rsqrt(jnp.mean(wide_rows * wide_rows, axis=-1, keepdims=True) + EPS)
        gathered[b, pl.ds(aligned(head * tokens + part * half, half), half), :] = (
            wide_rows * inv
        ).astype(BF16)

    barrier = pltpu.get_barrier_semaphore()

    def greet(to_view, to_head):
        pl.semaphore_signal(
            barrier, inc=1, device_id=(to_view, to_head), device_id_type=pl.DeviceIdType.MESH
        )

    def greet_z(d, carry):
        greet(x * NZ + (z + d) % NZ, head)
        return carry

    for to in (right, left, sib):
        greet(view, to)
    lax.fori_loop(1, NZ, greet_z, 0)
    for d in range(1, NX):
        greet(((x + d) % NX) * NZ + z, head)
    stream[...] = features[...]
    for b in range(BLOCKS):
        for j in range(3):
            qkv_w[b, pl.ds(aligned(view * 32, 32), 32), j * 128 : (j + 1) * 128] = attend[b, j]
            fast_w[b, j, x, z] = jnp.concatenate([fast[b, 0, j], fast[b, 1, j]], axis=1)
    normalize(0, 0)
    normalize(0, 1)
    pl.semaphore_wait(barrier, 3 + NZ - 1 + NX - 1)

    def tokens_of(b, of_head, part=None):
        if part is None:
            return gathered.at[b, pl.ds(aligned(of_head * tokens, tokens), tokens)]
        return gathered.at[b, pl.ds(aligned(of_head * tokens + part * half, half), half)]

    def send_tokens(b, of_head, part, recv, to, columns=None):
        piece = tokens_of(b, of_head, part)
        if columns is not None:
            piece = piece.at[:, columns]
        start_copy(piece, piece, g_send.at[b], g_recv.at[b, recv], view, to)

    def launch_tokens(b, part):
        send_tokens(b, head, part, part, right)
        send_tokens(b, head, part, 2 + part, left)
        send_tokens(b, head, part, 4, sib)

    def projections_z(b):
        rows = pl.ds(aligned(view * 32, 32), 32)
        for part, columns in enumerate(COLUMNS):
            own = qkv_w.at[b, rows, columns]

            def send(d, carry):
                to = x * NZ + (z + d) % NZ
                start_copy(own, own, w_send.at[b, part], w_recv.at[b, part], to, head)
                return carry

            lax.fori_loop(1, NZ, send, 0)

    def projections_x(b):
        rows = pl.ds(aligned(x * 256, 256), 256)
        for part, columns in enumerate(COLUMNS):
            wait_bytes(qkv_w.at[b, pl.ds(0, 32 * (NZ - 1)), columns], w_recv.at[b, part])
            own = qkv_w.at[b, rows, columns]
            for d in (1, 3, 2):
                to = ((x + d) % NX) * NZ + z
                start_copy(own, own, w_send.at[b, 2 + part], w_recv.at[b, 2 + part], to, head)

    def fast_x(b):
        own = fast_w.at[b, :, x, z]
        for d in (1, 3, 2):
            to = ((x + d) % NX) * NZ + z
            start_copy(own, own, w_send.at[b, 4], w_recv.at[b, 4], to, head)

    def fast_z(b):
        wait_bytes(fast_w.at[b, :, pl.ds(0, NX - 1), 0], w_recv.at[b, 4])
        own = fast_w.at[b, :, :, z]

        def send(d, carry):
            to = x * NZ + (z + d) % NZ
            start_copy(own, own, w_send.at[b, 5], w_recv.at[b, 5], to, head)
            return carry

        lax.fori_loop(1, NZ, send, 0)

    group = view // 4

    def output_fetch():
        rows = pl.ds(aligned(view * 32, 32), 32)
        target_group = (group - head + NH) % NH

        def send(i, carry):
            to = target_group * 4 + i

            @pl.when(to == view)
            def _():
                pltpu.make_async_copy(outw, out_w.at[:, rows], o_recv).start()

            @pl.when(to != view)
            def _():
                start_copy(outw, out_w.at[:, rows], o_send, o_recv, to, head)

            return carry

        lax.fori_loop(0, 4, send, 0)

    def output_rows(of_head):
        return pl.ds(aligned(((group + of_head) % NH) * 128, 128), 128)

    def output_share(b):
        own = out_w.at[b, output_rows(head)]
        for to in (right, left, opposite):
            start_copy(own, own, og_send.at[b], og_recv.at[b, 0], view, to)
        start_copy(own, own, og_send.at[b], og_recv.at[b, 1], view, sib)

    def output_forward(b):
        wait_bytes(out_w.at[b, pl.ds(0, 3 * 128)], og_recv.at[b, 0])
        for of_head in (right, left, opposite):
            piece = out_w.at[b, output_rows(of_head)]
            start_copy(piece, piece, og_send.at[b], og_recv.at[b, 1], view, sib)

    projections_z(0)
    launch_tokens(0, 0)
    launch_tokens(0, 1)
    fast_x(0)
    projections_x(0)
    fast_z(0)

    def block(b, carry):
        def project(s):
            @pl.when(s == 0)
            def _():
                wait_bytes(tokens_of(b, sib), g_recv.at[b, 4])
                for part, columns in enumerate(COLUMNS):
                    wait_bytes(qkv_w.at[b, pl.ds(0, 256 * (NX - 1)), columns], w_recv.at[b, 2 + part])

                @pl.when(b == 0)
                def _():
                    output_fetch()

            @pl.when(s == 1)
            def _():
                for part in range(2):
                    wait_bytes(tokens_of(b, left, part), g_recv.at[b, part])
                    send_tokens(b, left, part, 7 + part, right, slice(0, 512))
                    wait_bytes(tokens_of(b, right, part), g_recv.at[b, 2 + part])
                    send_tokens(b, right, part, 9 + part, left, slice(512, 1024))
                    send_tokens(b, right, part, 5, sib)
                    send_tokens(b, left, part, 6, sib)
                wait_bytes(tokens_of(b, sib), g_recv.at[b, 5])

            @pl.when(s == 2)
            def _():
                wait_bytes(tokens_of(b, sib), g_recv.at[b, 6])

            @pl.when(s == 3)
            def _():
                for part in range(2):
                    wait_bytes(tokens_of(b, opposite, part).at[:, 0:512], g_recv.at[b, 7 + part])
                    wait_bytes(tokens_of(b, opposite, part).at[:, 512:1024], g_recv.at[b, 9 + part])
                    send_tokens(b, opposite, part, 11, sib)
                wait_bytes(tokens_of(b, sib), g_recv.at[b, 11])

            rows = pl.ds(aligned(((y + gray(s)) % NY) * pair, pair), pair)
            packed = dot(gathered[b, rows, :], qkv_w[b]).astype(BF16)
            both = packed[:, 0:256].astype(F32)
            both = both * head_norm_wide(both)
            q = both[:, 0:128]
            v = packed[:, 256:384]
            queries[rows, :] = q.astype(BF16)
            scaled[rows, :] = (q * (SCORE_SCALE * math.log2(math.e))).astype(BF16)
            keys[rows, :] = both[:, 128:256].astype(BF16)
            low = low_lanes(v.shape)
            one = jnp.ones_like(v)
            values[0, rows, :] = jnp.where(low, v, one)
            values[1, rows, :] = jnp.where(low, one, v)

        def differentiate(s):
            @pl.when(s == 0)
            def _():
                wait_bytes(fast_w.at[b, :, :, pl.ds(0, NZ - 1)], w_recv.at[b, 5])

                @pl.when(b == 0)
                def _():
                    projections_z(1)
                    fast_x(1)

                total[...] = jnp.zeros_like(total)
                for j in range(3):
                    weights = fast_w[b, j].reshape(512, 128)
                    low = low_lanes(weights.shape)
                    wide[j, 0:512, :] = jnp.where(low, weights, jnp.zeros_like(weights))
                    wide[j, 512:1024, :] = jnp.where(low, jnp.zeros_like(weights), weights)

            rows = pl.ds(aligned(((y + gray(s)) % NY) * pair, pair), pair)
            k = keys[rows, :]
            low = low_lanes(k.shape)
            zero = jnp.zeros_like(k)
            sign = -mask[:, rows].astype(F32)
            for h in range(2):
                v = values[h, rows, :]
                kh = jnp.where(low, k, zero) if h == 0 else jnp.where(low, zero, k)
                vh = jnp.where(low, v, zero) if h == 0 else jnp.where(low, zero, v)
                f = slice(h * 512, h * 512 + 512)
                first = dot(wide[0, f, :], k, NT)
                third = dot(wide[1, f, :], k, NT)
                back = dot(wide[2, f, :], v, NT) * sign
                sigma = sigmoid(first)
                silu = first * sigma
                hidden = (silu * third * sign).astype(BF16)
                d_third = (back * silu).astype(BF16)
                d_first = (back * third * (sigma + silu * (1.0 - sigma))).astype(BF16)
                total[0] += dot(d_first, kh)
                total[1] += dot(d_third, kh)
                total[2] += dot(hidden, vh)

        def turn(u, carry):
            late = b + (1 - b) * (u // 4)
            s = late * (u // 2) + (1 - late) * (u % 2)
            kind = late * (u % 2) + (1 - late) * (u // 2)

            @pl.when(kind == 0)
            def _():
                project(s)

            @pl.when(kind == 1)
            def _():
                differentiate(s)

            return carry

        lax.fori_loop(0, 2 * NY, turn, 0)

        for j in range(3):
            to_sum[j * 512 : (j + 1) * 512, :] = total[j].astype(BF16)

        def along_x(source, target, sem):
            for d in (1, 3, 2):
                to = (x + d) % NX
                start_copy(
                    source(to), target(d - 1), r_send.at[b, sem], r_recv.at[b, sem], to * NZ + z, head
                )

        def along_z(source, target, sem):
            def send(d, carry):
                to = (z + d) % NZ
                start_copy(
                    source(to), target(d - 1), r_send.at[b, sem], r_recv.at[b, sem], x * NZ + to, head
                )
                return carry

            lax.fori_loop(1, NZ, send, 0)

        def rows_of(ref, start, count):
            return ref.at[pl.ds(aligned(start, 16), count)]

        def add(own, slots):
            return own.astype(F32) + jnp.sum(slots.astype(F32), axis=0)

        along_x(lambda to: rows_of(to_sum, to * 256, 256), lambda i: a_x.at[b, i], 0)
        along_z(lambda to: rows_of(to_sum, 1024 + to * 64, 64), lambda i: c_z.at[b, i], 1)

        @pl.when(b == 0)
        def _():
            wait_bytes(out_w.at[:, pl.ds(0, 128)], o_recv)

        output_share(b)

        def reduce_parts():
            wait_bytes(a_x.at[b], r_recv.at[b, 0])
            own = to_sum[pl.ds(aligned(x * 256, 16), 256), :]
            middle[0:256, :] = add(own, a_x[b]).astype(BF16)
            along_z(lambda to: rows_of(middle, to * 32, 32), lambda i: a_z.at[b, i], 2)
            wait_bytes(c_z.at[b], r_recv.at[b, 1])
            own = to_sum[pl.ds(aligned(1024 + z * 64, 16), 64), :]
            middle[256:320, :] = add(own, c_z[b]).astype(BF16)
            along_x(lambda to: rows_of(middle, 256 + to * 16, 16), lambda i: c_x.at[b, i], 3)

        def spread_parts():
            wait_bytes(a_z.at[b], r_recv.at[b, 2])
            mine = pl.ds(aligned(x * 256 + z * 32, 16), 32)
            own = middle[pl.ds(aligned(z * 32, 16), 32), :]
            summed[b, mine, :] = add(own, a_z[b]).astype(BF16)
            along_z(lambda to: summed.at[b, mine], lambda i: summed.at[b, mine], 4)
            wait_bytes(c_x.at[b], r_recv.at[b, 3])
            last = pl.ds(aligned(1024 + z * 64 + x * 16, 16), 16)
            own = middle[pl.ds(aligned(256 + x * 16, 16), 16), :]
            summed[b, last, :] = add(own, c_x[b]).astype(BF16)
            along_x(lambda to: summed.at[b, last], lambda i: summed.at[b, last], 5)

        def collect_parts():
            wait_bytes(summed.at[b, pl.ds(0, 32 * (NZ - 1))], r_recv.at[b, 4])
            mine = pl.ds(aligned(x * 256, 16), 256)
            along_x(lambda to: summed.at[b, mine], lambda i: summed.at[b, mine], 6)
            wait_bytes(summed.at[b, pl.ds(0, 16 * (NX - 1))], r_recv.at[b, 5])
            last = pl.ds(aligned(1024 + z * 64, 16), 64)
            along_z(lambda to: summed.at[b, last], lambda i: summed.at[b, last], 7)

        def attend_rows(i, carry):
            @pl.when(i == 1)
            def _():
                reduce_parts()

            rows = pl.ds(aligned(i * 1024, 1024), 1024)
            q = scaled[rows, :]
            low = low_lanes(q.shape)
            zero = jnp.zeros_like(q)
            own = [jnp.where(low, q, zero), jnp.where(low, zero, q)]
            weighted = [jnp.zeros(q.shape, F32)] * 2
            for part in range(length // 256):
                at = slice(part * 256, (part + 1) * 256)
                for h in range(2):
                    expo = jnp.exp2(dot(own[h], keys[at, :], NT)).astype(BF16)
                    weighted[h] = weighted[h] + dot(expo, values[h, at, :])
            out = [each / pltpu.roll(each, 64, 1) for each in weighted]
            attended[rows, :] = jnp.where(low_lanes(out[0].shape), out[0], out[1])
            return carry

        lax.fori_loop(0, length // 1024, attend_rows, 0)
        spread_parts()
        output_forward(b)
        collect_parts()

        wait_bytes(summed.at[b, pl.ds(0, 256 * (NX - 1))], r_recv.at[b, 6])
        wait_bytes(summed.at[b, pl.ds(0, 64 * (NZ - 1))], r_recv.at[b, 7])

        @pl.when(b == 0)
        def _():
            projections_x(1)
            fast_z(1)

        row = lax.broadcasted_iota(jnp.int32, (128, 128), 0)
        col = lax.broadcasted_iota(jnp.int32, (128, 128), 1)
        same = (row < 64) == (col < 64)
        eye = row == col
        grams, scales = [], []
        for j in range(3):
            gradient = summed[b, j * 512 : (j + 1) * 512, :]
            gram = jnp.where(same, dot(gradient, gradient, TN), 0.0)
            diagonal = jnp.where(eye, gram, 0.0)
            squares = jnp.sum(jnp.where(same, jnp.sum(diagonal, axis=1, keepdims=True), 0.0), axis=0, keepdims=True)
            scale = lax.rsqrt(squares + 1e-06)
            scales.append(scale)
            grams.append(gram * (scale * scale))
        for step in range(NS_STEPS):
            product = exact if step < 2 else triple
            polys = [
                jnp.where(eye, NEWTON[0], 0.0)
                + NEWTON[1] * gram
                + NEWTON[2] * product(gram, gram)
                for gram in grams
            ]
            if step < NS_STEPS - 1:
                halves = [product(poly, gram) for poly, gram in zip(polys, grams)]
                grams = [product(each, poly) for each, poly in zip(halves, polys)]
            if step == 0:
                chains = polys
            else:
                chains = [triple(poly, chain) for poly, chain in zip(polys, chains)]
        for j in range(3):
            gradient = summed[b, j * 512 : (j + 1) * 512, :]
            upper, lower = split(chains[j])
            current = (dot(gradient, upper) + dot(gradient, lower)) * scales[j]
            updated = (fast_w[b, j].reshape(512, 128).astype(F32) - LEARN_RATE * current).astype(BF16)
            low = low_lanes(updated.shape)
            wide[j, 0:512, :] = jnp.where(low, updated, jnp.zeros_like(updated))
            wide[j, 512:1024, :] = jnp.where(low, jnp.zeros_like(updated), updated)

        def apply_rows(u, carry):
            part, s = u // NY, u % NY
            chip = (y + gray(NY - 1 - s)) % NY
            near = pl.ds(aligned((chip * 2 + core) * tokens + part * half, half), half)
            far = pl.ds(aligned((chip * 2 + 1 - core) * tokens + part * half, half), half)
            q = jnp.concatenate([queries[far, :], queries[near, :]], axis=0)
            applied = jnp.zeros(q.shape, F32)
            for block_f in range(2):
                f = slice(block_f * 512, block_f * 512 + 512)
                first = dot(q, wide[0, f, :], NT)
                third = dot(q, wide[1, f, :], NT)
                hidden = (first * sigmoid(first) * third).astype(BF16)
                applied = applied + dot(hidden, wide[2, f, :])
            applied = applied * head_norm(applied)
            to_mix[far, :] = (attended[far, :] + applied[0:half]).astype(BF16)
            to_mix[near, :] = (attended[near, :] + applied[half:]).astype(BF16)
            target = mixed.at[
                b, pl.ds(aligned(part * half, half), half), pl.ds(aligned(head * 128, 128), 128)
            ]
            sems = m_send.at[b], m_recv.at[b, part]
            start_copy(to_mix.at[far], target, *sems, view, chip * 2 + 1 - core)

            @pl.when(s < NY - 1)
            def _():
                start_copy(to_mix.at[near], target, *sems, view, chip * 2 + core)

            @pl.when(s == NY - 1)
            def _():
                target[...] = to_mix[near, :]

            return carry

        lax.fori_loop(0, 2 * NY, apply_rows, 0)

        wait_bytes(out_w.at[b, pl.ds(0, 4 * 128)], og_recv.at[b, 1])
        for part in range(2):
            rows = slice(part * half, (part + 1) * half)
            wait_bytes(mixed.at[b, rows, pl.ds(0, 128 * (NH - 1))], m_recv.at[b, part])
            projected = dot(mixed[b, rows, :], out_w[b])
            stream[rows, :] = (stream[rows, :].astype(F32) + projected).astype(BF16)

            @pl.when(b < BLOCKS - 1)
            def _():
                normalize(b + 1, part)
                launch_tokens(b + 1, part)

        wait_bytes(to_mix.at[pl.ds(0, tokens * (NH - 1))], m_send.at[b])
        for sem, count in enumerate((768, 448, 224, 48, 224, 48, 768, 448)):
            wait_bytes(summed.at[b, pl.ds(0, count)], r_send.at[b, sem])
        wait_bytes(gathered.at[b, pl.ds(0, tokens * 7)], g_send.at[b])
        wait_bytes(out_w.at[b, pl.ds(0, 128 * 7)], og_send.at[b])
        return carry

    lax.fori_loop(0, BLOCKS, block, 0)
    result[...] = stream[...]

    for b in range(BLOCKS):
        for part, columns in enumerate(COLUMNS):
            wait_bytes(qkv_w.at[b, pl.ds(0, 32 * (NZ - 1)), columns], w_send.at[b, part])
            wait_bytes(qkv_w.at[b, pl.ds(0, 256 * (NX - 1)), columns], w_send.at[b, 2 + part])
        wait_bytes(fast_w.at[b, :, pl.ds(0, NX - 1), 0], w_send.at[b, 4])
        wait_bytes(fast_w.at[b, :, :, pl.ds(0, NZ - 1)], w_send.at[b, 5])

    @pl.when(head == 0)
    def _():
        wait_bytes(out_w.at[:, pl.ds(0, 96)], o_send)

    @pl.when(head != 0)
    def _():
        wait_bytes(out_w.at[:, pl.ds(0, 128)], o_send)


def shards(features, attend_weight, output_weight, fast_init, update_mask):
    tokens, width = features.shape
    length = tokens * NH
    vmem = pl.BlockSpec(memory_space=pltpu.VMEM)
    dma = pltpu.SemaphoreType.DMA
    return pl.pallas_call(
        kernel,
        out_shape=jax.ShapeDtypeStruct((tokens, width), BF16),
        in_specs=[vmem] * 5,
        out_specs=vmem,
        scratch_shapes=[
            pltpu.VMEM((tokens, width), BF16),
            pltpu.VMEM((BLOCKS, length, width), BF16),
            pltpu.VMEM((BLOCKS, width, 384), BF16),
            pltpu.VMEM((BLOCKS, 3, NX, NZ, 16, 128), BF16),
            pltpu.VMEM((BLOCKS, width, width), BF16),
            pltpu.VMEM((length, 128), BF16),
            pltpu.VMEM((length, 128), BF16),
            pltpu.VMEM((length, 128), BF16),
            pltpu.VMEM((2, length, 128), BF16),
            pltpu.VMEM((3, 1024, 128), BF16),
            pltpu.VMEM((3, 512, 128), F32),
            pltpu.VMEM((1536, 128), BF16),
            pltpu.VMEM((BLOCKS, NX - 1, 256, 128), BF16),
            pltpu.VMEM((BLOCKS, NZ - 1, 64, 128), BF16),
            pltpu.VMEM((BLOCKS, NZ - 1, 32, 128), BF16),
            pltpu.VMEM((BLOCKS, NX - 1, 16, 128), BF16),
            pltpu.VMEM((320, 128), BF16),
            pltpu.VMEM((BLOCKS, 1536, 128), BF16),
            pltpu.VMEM((length, 128), F32),
            pltpu.VMEM((length, 128), BF16),
            pltpu.VMEM((BLOCKS, tokens, width), BF16),
            dma((BLOCKS, 6)),
            dma((BLOCKS, 6)),
            dma,
            dma,
            dma((BLOCKS, 2)),
            dma((BLOCKS,)),
            dma((BLOCKS, 12)),
            dma((BLOCKS,)),
            dma((BLOCKS, 8)),
            dma((BLOCKS, 8)),
            dma((BLOCKS, 2)),
            dma((BLOCKS,)),
        ],
        compiler_params=pltpu.CompilerParams(
            collective_id=0, has_side_effects=True, vmem_limit_bytes=56 * 1024 * 1024
        ),
        name="lact",
    )(features, attend_weight, jnp.swapaxes(fast_init, 3, 4), output_weight, update_mask)


def solution(mesh):
    return jax.shard_map(
        shards,
        mesh=mesh,
        in_specs=(
            P(("view", "head"), None),
            P(None, None, "view", "head"),
            P(None, "view", None),
            P(None, "head", None, None, "view"),
            P("view", None),
        ),
        out_specs=P(("view", "head"), None),
        check_vma=False,
    )
```

```python
import math

import jax
import jax.numpy as jnp
from jax import lax
from jax.experimental import pallas as pl
from jax.experimental.pallas import tpu as pltpu
from jax.sharding import PartitionSpec as P

BLOCKS = 2
NS_STEPS = 5
NEWTON = (3.4445, -4.775, 2.0315)
LEARN_RATE = 1.0
SCORE_SCALE = 0.25
EPS = 1e-05

NX, NZ, NY = 4, 8, 4
NV, NH = NX * NZ, 2 * NY

COLUMNS = (slice(0, 128), slice(128, 384))

F32 = jnp.float32
BF16 = jnp.bfloat16
NT = (((1,), (1,)), ((), ()))
TN = (((0,), (0,)), ((), ()))


def dot(a, b, dims=(((1,), (0,)), ((), ())), precision=None):
    return lax.dot_general(a, b, dims, precision=precision, preferred_element_type=F32)


def low_lanes(shape):
    return lax.broadcasted_iota(jnp.int32, shape, len(shape) - 1) < 64


def head_norm(x):
    low = low_lanes(x.shape)
    sq = x * x
    first = jnp.sum(jnp.where(low, sq, 0.0), axis=-1, keepdims=True)
    second = jnp.sum(jnp.where(low, 0.0, sq), axis=-1, keepdims=True)
    return lax.rsqrt(jnp.where(low, first, second) * (1.0 / 64) + EPS)


def split(x):
    upper = x.astype(BF16)
    return upper, (x - upper.astype(F32)).astype(BF16)


def head_norm_wide(x):
    upper, lower = split(x * x)
    row = lax.broadcasted_iota(jnp.int32, (x.shape[1], x.shape[1]), 0) // 64
    col = lax.broadcasted_iota(jnp.int32, (x.shape[1], x.shape[1]), 1) // 64
    ones = jnp.where(row == col, 1.0, 0.0).astype(BF16)
    return lax.rsqrt((dot(upper, ones) + dot(lower, ones)) * (1.0 / 64) + EPS)


def exact(a, b):
    return dot(a, b, precision=lax.Precision.HIGHEST)


def triple(a, b):
    a_upper, a_lower = split(a)
    b_upper, b_lower = split(b)
    return dot(a_upper, b_upper) + (dot(a_upper, b_lower) + dot(a_lower, b_upper))


def sigmoid(x):
    return 0.5 + 0.5 * jnp.tanh(0.5 * x)


def gray(p):
    return p + (p // 2) * (1 - 2 * (p % 2))


def start_copy(src, dst, send, recv, view, head):
    pltpu.make_async_remote_copy(
        src_ref=src,
        dst_ref=dst,
        send_sem=send,
        recv_sem=recv,
        device_id=(view, head),
        device_id_type=pl.DeviceIdType.MESH,
    ).start()


def wait_bytes(ref, sem):
    pltpu.make_async_copy(ref, ref, sem).wait()


def kernel(
    features,
    attend,
    fast,
    outw,
    mask,
    result,
    stream,
    gathered,
    qkv_w,
    fast_w,
    out_w,
    queries,
    scaled,
    keys,
    values,
    wide,
    total,
    to_sum,
    a_x,
    c_z,
    a_z,
    c_x,
    middle,
    summed,
    attended,
    to_mix,
    mixed,
    w_recv,
    w_send,
    o_recv,
    o_send,
    og_recv,
    og_send,
    g_recv,
    g_send,
    r_recv,
    r_send,
    m_recv,
    m_send,
):
    view, head = lax.axis_index("view"), lax.axis_index("head")
    x, z = view // NZ, view % NZ
    y, core = head // 2, head % 2
    tokens = stream.shape[0]
    length = tokens * NH
    sib = y * 2 + (1 - core)
    right = ((y + 1) % NY) * 2 + core
    left = ((y + NY - 1) % NY) * 2 + core
    opposite = ((y + 2) % NY) * 2 + core
    half = tokens // 2
    pair = tokens * 2

    def aligned(value, to):
        return pl.multiple_of(value, to)

    def normalize(b, part):
        rows = slice(part * half, (part + 1) * half)
        wide_rows = stream[rows, :].astype(F32)
        inv = lax.rsqrt(jnp.mean(wide_rows * wide_rows, axis=-1, keepdims=True) + EPS)
        gathered[b, pl.ds(aligned(head * tokens + part * half, half), half), :] = (
            wide_rows * inv
        ).astype(BF16)

    barrier = pltpu.get_barrier_semaphore()

    def greet(to_view, to_head):
        pl.semaphore_signal(
            barrier, inc=1, device_id=(to_view, to_head), device_id_type=pl.DeviceIdType.MESH
        )

    def greet_z(d, carry):
        greet(x * NZ + (z + d) % NZ, head)
        return carry

    for to in (right, left, sib):
        greet(view, to)
    lax.fori_loop(1, NZ, greet_z, 0)
    for d in range(1, NX):
        greet(((x + d) % NX) * NZ + z, head)
    stream[...] = features[...]
    for b in range(BLOCKS):
        for j in range(3):
            qkv_w[b, pl.ds(aligned(view * 32, 32), 32), j * 128 : (j + 1) * 128] = attend[b, j]
            fast_w[b, j, x, z] = jnp.concatenate([fast[b, 0, j], fast[b, 1, j]], axis=1)
    normalize(0, 0)
    normalize(0, 1)
    pl.semaphore_wait(barrier, 3 + NZ - 1 + NX - 1)

    def tokens_of(b, of_head, part=None):
        if part is None:
            return gathered.at[b, pl.ds(aligned(of_head * tokens, tokens), tokens)]
        return gathered.at[b, pl.ds(aligned(of_head * tokens + part * half, half), half)]

    def send_tokens(b, of_head, part, recv, to, columns=None):
        piece = tokens_of(b, of_head, part)
        if columns is not None:
            piece = piece.at[:, columns]
        start_copy(piece, piece, g_send.at[b], g_recv.at[b, recv], view, to)

    def launch_tokens(b, part):
        send_tokens(b, head, part, part, right)
        send_tokens(b, head, part, 2 + part, left)
        send_tokens(b, head, part, 4, sib)

    def projections_z(b):
        rows = pl.ds(aligned(view * 32, 32), 32)
        for part, columns in enumerate(COLUMNS):
            own = qkv_w.at[b, rows, columns]

            def send(d, carry):
                to = x * NZ + (z + d) % NZ
                start_copy(own, own, w_send.at[b, part], w_recv.at[b, part], to, head)
                return carry

            lax.fori_loop(1, NZ, send, 0)

    def projections_x(b):
        rows = pl.ds(aligned(x * 256, 256), 256)
        for part, columns in enumerate(COLUMNS):
            wait_bytes(qkv_w.at[b, pl.ds(0, 32 * (NZ - 1)), columns], w_recv.at[b, part])
            own = qkv_w.at[b, rows, columns]
            for d in (1, 3, 2):
                to = ((x + d) % NX) * NZ + z
                start_copy(own, own, w_send.at[b, 2 + part], w_recv.at[b, 2 + part], to, head)

    def fast_x(b):
        own = fast_w.at[b, :, x, z]
        for d in (1, 3, 2):
            to = ((x + d) % NX) * NZ + z
            start_copy(own, own, w_send.at[b, 4], w_recv.at[b, 4], to, head)

    def fast_z(b):
        wait_bytes(fast_w.at[b, :, pl.ds(0, NX - 1), 0], w_recv.at[b, 4])
        own = fast_w.at[b, :, :, z]

        def send(d, carry):
            to = x * NZ + (z + d) % NZ
            start_copy(own, own, w_send.at[b, 5], w_recv.at[b, 5], to, head)
            return carry

        lax.fori_loop(1, NZ, send, 0)

    group = view // 4

    def output_fetch():
        rows = pl.ds(aligned(view * 32, 32), 32)
        target_group = (group - head + NH) % NH

        def send(i, carry):
            to = target_group * 4 + i

            @pl.when(to == view)
            def _():
                pltpu.make_async_copy(outw, out_w.at[:, rows], o_recv).start()

            @pl.when(to != view)
            def _():
                start_copy(outw, out_w.at[:, rows], o_send, o_recv, to, head)

            return carry

        lax.fori_loop(0, 4, send, 0)

    def output_rows(of_head):
        return pl.ds(aligned(((group + of_head) % NH) * 128, 128), 128)

    def output_share(b):
        own = out_w.at[b, output_rows(head)]
        for to in (right, left, opposite):
            start_copy(own, own, og_send.at[b], og_recv.at[b, 0], view, to)
        start_copy(own, own, og_send.at[b], og_recv.at[b, 1], view, sib)

    def output_forward(b):
        wait_bytes(out_w.at[b, pl.ds(0, 3 * 128)], og_recv.at[b, 0])
        for of_head in (right, left, opposite):
            piece = out_w.at[b, output_rows(of_head)]
            start_copy(piece, piece, og_send.at[b], og_recv.at[b, 1], view, sib)

    projections_z(0)
    launch_tokens(0, 0)
    launch_tokens(0, 1)
    fast_x(0)
    projections_x(0)
    fast_z(0)

    def block(b, carry):
        def forward_opposite(part):
            wait_bytes(tokens_of(b, opposite, part).at[:, 0:512], g_recv.at[b, 7 + part])
            wait_bytes(tokens_of(b, opposite, part).at[:, 512:1024], g_recv.at[b, 9 + part])
            send_tokens(b, opposite, part, 11, sib)

        def project(s):
            @pl.when(s == b)
            def _():
                for part in range(2):
                    wait_bytes(tokens_of(b, left, part), g_recv.at[b, part])
                    send_tokens(b, left, part, 7 + part, right, slice(0, 512))
                    wait_bytes(tokens_of(b, right, part), g_recv.at[b, 2 + part])
                    send_tokens(b, right, part, 9 + part, left, slice(512, 1024))
                    send_tokens(b, right, part, 5, sib)
                    send_tokens(b, left, part, 6, sib)

            @pl.when(s == 0)
            def _():
                wait_bytes(tokens_of(b, sib), g_recv.at[b, 4])
                for part, columns in enumerate(COLUMNS):
                    wait_bytes(qkv_w.at[b, pl.ds(0, 256 * (NX - 1)), columns], w_recv.at[b, 2 + part])

                @pl.when(b == 0)
                def _():
                    output_fetch()

            @pl.when(s == 1)
            def _():
                wait_bytes(tokens_of(b, sib), g_recv.at[b, 5])

            @pl.when(s == 2)
            def _():
                wait_bytes(tokens_of(b, sib), g_recv.at[b, 6])

            @pl.when(s == 3)
            def _():
                forward_opposite(1)
                wait_bytes(tokens_of(b, sib), g_recv.at[b, 11])

            rows = pl.ds(aligned(((y + gray(s)) % NY) * pair, pair), pair)
            packed = dot(gathered[b, rows, :], qkv_w[b]).astype(BF16)
            both = packed[:, 0:256].astype(F32)
            both = both * head_norm_wide(both)
            q = both[:, 0:128]
            v = packed[:, 256:384]
            queries[rows, :] = q.astype(BF16)
            scaled[rows, :] = (q * (SCORE_SCALE * math.log2(math.e))).astype(BF16)
            keys[rows, :] = both[:, 128:256].astype(BF16)
            low = low_lanes(v.shape)
            one = jnp.ones_like(v)
            values[0, rows, :] = jnp.where(low, v, one)
            values[1, rows, :] = jnp.where(low, one, v)

        def differentiate(s):
            @pl.when(s == 0)
            def _():
                wait_bytes(fast_w.at[b, :, :, pl.ds(0, NZ - 1)], w_recv.at[b, 5])

                @pl.when(b == 0)
                def _():
                    projections_z(1)
                    fast_x(1)

                total[...] = jnp.zeros_like(total)
                for j in range(3):
                    weights = fast_w[b, j].reshape(512, 128)
                    low = low_lanes(weights.shape)
                    wide[j, 0:512, :] = jnp.where(low, weights, jnp.zeros_like(weights))
                    wide[j, 512:1024, :] = jnp.where(low, jnp.zeros_like(weights), weights)

            @pl.when(s == 2)
            def _():
                forward_opposite(0)

            rows = pl.ds(aligned(((y + gray(s)) % NY) * pair, pair), pair)
            k = keys[rows, :]
            low = low_lanes(k.shape)
            zero = jnp.zeros_like(k)
            sign = -mask[:, rows].astype(F32)
            for h in range(2):
                v = values[h, rows, :]
                kh = jnp.where(low, k, zero) if h == 0 else jnp.where(low, zero, k)
                vh = jnp.where(low, v, zero) if h == 0 else jnp.where(low, zero, v)
                f = slice(h * 512, h * 512 + 512)
                first = dot(wide[0, f, :], k, NT)
                third = dot(wide[1, f, :], k, NT)
                back = dot(wide[2, f, :], v, NT) * sign
                sigma = sigmoid(first)
                silu = first * sigma
                hidden = (silu * third * sign).astype(BF16)
                d_third = (back * silu).astype(BF16)
                d_first = (back * third * (sigma + silu * (1.0 - sigma))).astype(BF16)
                total[0] += dot(d_first, kh)
                total[1] += dot(d_third, kh)
                total[2] += dot(hidden, vh)

        def turn(u, carry):
            late = b + (1 - b) * (u // 4)
            s = late * (u // 2) + (1 - late) * (u % 2)
            kind = late * (u % 2) + (1 - late) * (u // 2)

            @pl.when(kind == 0)
            def _():
                project(s)

            @pl.when(kind == 1)
            def _():
                differentiate(s)

            return carry

        lax.fori_loop(0, 2 * NY, turn, 0)

        for j in range(3):
            to_sum[j * 512 : (j + 1) * 512, :] = total[j].astype(BF16)

        def along_x(source, target, sem):
            for d in (1, 3, 2):
                to = (x + d) % NX
                start_copy(
                    source(to), target(d - 1), r_send.at[b, sem], r_recv.at[b, sem], to * NZ + z, head
                )

        def along_z(source, target, sem):
            def send(d, carry):
                to = (z + d) % NZ
                start_copy(
                    source(to), target(d - 1), r_send.at[b, sem], r_recv.at[b, sem], x * NZ + to, head
                )
                return carry

            lax.fori_loop(1, NZ, send, 0)

        def rows_of(ref, start, count):
            return ref.at[pl.ds(aligned(start, 16), count)]

        def add(own, slots):
            return own.astype(F32) + jnp.sum(slots.astype(F32), axis=0)

        along_x(lambda to: rows_of(to_sum, to * 256, 256), lambda i: a_x.at[b, i], 0)
        along_z(lambda to: rows_of(to_sum, 1024 + to * 64, 64), lambda i: c_z.at[b, i], 1)

        @pl.when(b == 0)
        def _():
            wait_bytes(out_w.at[:, pl.ds(0, 128)], o_recv)

        output_share(b)

        def reduce_parts():
            wait_bytes(a_x.at[b], r_recv.at[b, 0])
            own = to_sum[pl.ds(aligned(x * 256, 16), 256), :]
            middle[0:256, :] = add(own, a_x[b]).astype(BF16)
            along_z(lambda to: rows_of(middle, to * 32, 32), lambda i: a_z.at[b, i], 2)
            wait_bytes(c_z.at[b], r_recv.at[b, 1])
            own = to_sum[pl.ds(aligned(1024 + z * 64, 16), 64), :]
            middle[256:320, :] = add(own, c_z[b]).astype(BF16)
            along_x(lambda to: rows_of(middle, 256 + to * 16, 16), lambda i: c_x.at[b, i], 3)

        def spread_parts():
            wait_bytes(a_z.at[b], r_recv.at[b, 2])
            mine = pl.ds(aligned(x * 256 + z * 32, 16), 32)
            own = middle[pl.ds(aligned(z * 32, 16), 32), :]
            summed[b, mine, :] = add(own, a_z[b]).astype(BF16)
            along_z(lambda to: summed.at[b, mine], lambda i: summed.at[b, mine], 4)
            wait_bytes(c_x.at[b], r_recv.at[b, 3])
            last = pl.ds(aligned(1024 + z * 64 + x * 16, 16), 16)
            own = middle[pl.ds(aligned(256 + x * 16, 16), 16), :]
            summed[b, last, :] = add(own, c_x[b]).astype(BF16)
            along_x(lambda to: summed.at[b, last], lambda i: summed.at[b, last], 5)

        def collect_parts():
            wait_bytes(summed.at[b, pl.ds(0, 32 * (NZ - 1))], r_recv.at[b, 4])
            mine = pl.ds(aligned(x * 256, 16), 256)
            along_x(lambda to: summed.at[b, mine], lambda i: summed.at[b, mine], 6)
            wait_bytes(summed.at[b, pl.ds(0, 16 * (NX - 1))], r_recv.at[b, 5])
            last = pl.ds(aligned(1024 + z * 64, 16), 64)
            along_z(lambda to: summed.at[b, last], lambda i: summed.at[b, last], 7)

        def attend_rows(i, carry):
            @pl.when(i == 1)
            def _():
                reduce_parts()

            rows = pl.ds(aligned(i * 1024, 1024), 1024)
            q = scaled[rows, :]
            low = low_lanes(q.shape)
            zero = jnp.zeros_like(q)
            own = [jnp.where(low, q, zero), jnp.where(low, zero, q)]
            weighted = [jnp.zeros(q.shape, F32)] * 2
            for part in range(length // 256):
                at = slice(part * 256, (part + 1) * 256)
                for h in range(2):
                    expo = jnp.exp2(dot(own[h], keys[at, :], NT)).astype(BF16)
                    weighted[h] = weighted[h] + dot(expo, values[h, at, :])
            out = [each / pltpu.roll(each, 64, 1) for each in weighted]
            attended[rows, :] = jnp.where(low_lanes(out[0].shape), out[0], out[1])
            return carry

        lax.fori_loop(0, length // 1024, attend_rows, 0)
        spread_parts()
        output_forward(b)
        collect_parts()

        wait_bytes(summed.at[b, pl.ds(0, 256 * (NX - 1))], r_recv.at[b, 6])
        wait_bytes(summed.at[b, pl.ds(0, 64 * (NZ - 1))], r_recv.at[b, 7])

        @pl.when(b == 0)
        def _():
            projections_x(1)
            fast_z(1)

        row = lax.broadcasted_iota(jnp.int32, (128, 128), 0)
        col = lax.broadcasted_iota(jnp.int32, (128, 128), 1)
        same = (row < 64) == (col < 64)
        eye = row == col
        grams, scales = [], []
        for j in range(3):
            gradient = summed[b, j * 512 : (j + 1) * 512, :]
            gram = jnp.where(same, dot(gradient, gradient, TN), 0.0)
            diagonal = jnp.where(eye, gram, 0.0)
            squares = jnp.sum(jnp.where(same, jnp.sum(diagonal, axis=1, keepdims=True), 0.0), axis=0, keepdims=True)
            scale = lax.rsqrt(squares + 1e-06)
            scales.append(scale)
            grams.append(gram * (scale * scale))
        for step in range(NS_STEPS):
            product = exact if step < 2 else triple
            polys = [
                jnp.where(eye, NEWTON[0], 0.0)
                + NEWTON[1] * gram
                + NEWTON[2] * product(gram, gram)
                for gram in grams
            ]
            if step < NS_STEPS - 1:
                halves = [product(poly, gram) for poly, gram in zip(polys, grams)]
                grams = [product(each, poly) for each, poly in zip(halves, polys)]
            if step == 0:
                chains = polys
            else:
                chains = [triple(poly, chain) for poly, chain in zip(polys, chains)]
        for j in range(3):
            gradient = summed[b, j * 512 : (j + 1) * 512, :]
            upper, lower = split(chains[j])
            current = (dot(gradient, upper) + dot(gradient, lower)) * scales[j]
            updated = (fast_w[b, j].reshape(512, 128).astype(F32) - LEARN_RATE * current).astype(BF16)
            low = low_lanes(updated.shape)
            wide[j, 0:512, :] = jnp.where(low, updated, jnp.zeros_like(updated))
            wide[j, 512:1024, :] = jnp.where(low, jnp.zeros_like(updated), updated)

        def apply_rows(u, carry):
            part, s = u // NY, u % NY
            chip = (y + gray(NY - 1 - s)) % NY
            near = pl.ds(aligned((chip * 2 + core) * tokens + part * half, half), half)
            far = pl.ds(aligned((chip * 2 + 1 - core) * tokens + part * half, half), half)
            q = jnp.concatenate([queries[far, :], queries[near, :]], axis=0)
            applied = jnp.zeros(q.shape, F32)
            for block_f in range(2):
                f = slice(block_f * 512, block_f * 512 + 512)
                first = dot(q, wide[0, f, :], NT)
                third = dot(q, wide[1, f, :], NT)
                hidden = (first * sigmoid(first) * third).astype(BF16)
                applied = applied + dot(hidden, wide[2, f, :])
            applied = applied * head_norm(applied)
            to_mix[far, :] = (attended[far, :] + applied[0:half]).astype(BF16)
            to_mix[near, :] = (attended[near, :] + applied[half:]).astype(BF16)
            target = mixed.at[
                b, pl.ds(aligned(part * half, half), half), pl.ds(aligned(head * 128, 128), 128)
            ]
            sems = m_send.at[b], m_recv.at[b, part]
            start_copy(to_mix.at[far], target, *sems, view, chip * 2 + 1 - core)

            @pl.when(s < NY - 1)
            def _():
                start_copy(to_mix.at[near], target, *sems, view, chip * 2 + core)

            @pl.when(s == NY - 1)
            def _():
                target[...] = to_mix[near, :]

            return carry

        lax.fori_loop(0, 2 * NY, apply_rows, 0)

        wait_bytes(out_w.at[b, pl.ds(0, 4 * 128)], og_recv.at[b, 1])
        for part in range(2):
            rows = slice(part * half, (part + 1) * half)
            wait_bytes(mixed.at[b, rows, pl.ds(0, 128 * (NH - 1))], m_recv.at[b, part])
            projected = dot(mixed[b, rows, :], out_w[b])
            stream[rows, :] = (stream[rows, :].astype(F32) + projected).astype(BF16)

            @pl.when(b < BLOCKS - 1)
            def _():
                normalize(b + 1, part)
                launch_tokens(b + 1, part)

        wait_bytes(to_mix.at[pl.ds(0, tokens * (NH - 1))], m_send.at[b])
        for sem, count in enumerate((768, 448, 224, 48, 224, 48, 768, 448)):
            wait_bytes(summed.at[b, pl.ds(0, count)], r_send.at[b, sem])
        wait_bytes(gathered.at[b, pl.ds(0, tokens * 7)], g_send.at[b])
        wait_bytes(out_w.at[b, pl.ds(0, 128 * 7)], og_send.at[b])
        return carry

    lax.fori_loop(0, BLOCKS, block, 0)
    result[...] = stream[...]

    for b in range(BLOCKS):
        for part, columns in enumerate(COLUMNS):
            wait_bytes(qkv_w.at[b, pl.ds(0, 32 * (NZ - 1)), columns], w_send.at[b, part])
            wait_bytes(qkv_w.at[b, pl.ds(0, 256 * (NX - 1)), columns], w_send.at[b, 2 + part])
        wait_bytes(fast_w.at[b, :, pl.ds(0, NX - 1), 0], w_send.at[b, 4])
        wait_bytes(fast_w.at[b, :, :, pl.ds(0, NZ - 1)], w_send.at[b, 5])

    @pl.when(head == 0)
    def _():
        wait_bytes(out_w.at[:, pl.ds(0, 96)], o_send)

    @pl.when(head != 0)
    def _():
        wait_bytes(out_w.at[:, pl.ds(0, 128)], o_send)


def shards(features, attend_weight, output_weight, fast_init, update_mask):
    tokens, width = features.shape
    length = tokens * NH
    vmem = pl.BlockSpec(memory_space=pltpu.VMEM)
    dma = pltpu.SemaphoreType.DMA
    return pl.pallas_call(
        kernel,
        out_shape=jax.ShapeDtypeStruct((tokens, width), BF16),
        in_specs=[vmem] * 5,
        out_specs=vmem,
        scratch_shapes=[
            pltpu.VMEM((tokens, width), BF16),
            pltpu.VMEM((BLOCKS, length, width), BF16),
            pltpu.VMEM((BLOCKS, width, 384), BF16),
            pltpu.VMEM((BLOCKS, 3, NX, NZ, 16, 128), BF16),
            pltpu.VMEM((BLOCKS, width, width), BF16),
            pltpu.VMEM((length, 128), BF16),
            pltpu.VMEM((length, 128), BF16),
            pltpu.VMEM((length, 128), BF16),
            pltpu.VMEM((2, length, 128), BF16),
            pltpu.VMEM((3, 1024, 128), BF16),
            pltpu.VMEM((3, 512, 128), F32),
            pltpu.VMEM((1536, 128), BF16),
            pltpu.VMEM((BLOCKS, NX - 1, 256, 128), BF16),
            pltpu.VMEM((BLOCKS, NZ - 1, 64, 128), BF16),
            pltpu.VMEM((BLOCKS, NZ - 1, 32, 128), BF16),
            pltpu.VMEM((BLOCKS, NX - 1, 16, 128), BF16),
            pltpu.VMEM((320, 128), BF16),
            pltpu.VMEM((BLOCKS, 1536, 128), BF16),
            pltpu.VMEM((length, 128), F32),
            pltpu.VMEM((length, 128), BF16),
            pltpu.VMEM((BLOCKS, tokens, width), BF16),
            dma((BLOCKS, 6)),
            dma((BLOCKS, 6)),
            dma,
            dma,
            dma((BLOCKS, 2)),
            dma((BLOCKS,)),
            dma((BLOCKS, 12)),
            dma((BLOCKS,)),
            dma((BLOCKS, 8)),
            dma((BLOCKS, 8)),
            dma((BLOCKS, 2)),
            dma((BLOCKS,)),
        ],
        compiler_params=pltpu.CompilerParams(
            collective_id=0, has_side_effects=True, vmem_limit_bytes=56 * 1024 * 1024
        ),
        name="lact",
    )(features, attend_weight, jnp.swapaxes(fast_init, 3, 4), output_weight, update_mask)


def solution(mesh):
    return jax.shard_map(
        shards,
        mesh=mesh,
        in_specs=(
            P(("view", "head"), None),
            P(None, None, "view", "head"),
            P(None, "view", None),
            P(None, "head", None, None, "view"),
            P("view", None),
        ),
        out_specs=P(("view", "head"), None),
        check_vma=False,
    )
```

```python
import math

import jax
import jax.numpy as jnp
from jax import lax
from jax.experimental import pallas as pl
from jax.experimental.pallas import tpu as pltpu
from jax.sharding import PartitionSpec as P

BLOCKS = 2
NS_STEPS = 5
NEWTON = (3.4445, -4.775, 2.0315)
LEARN_RATE = 1.0
SCORE_SCALE = 0.25
EPS = 1e-05

NX, NZ, NY = 4, 8, 4
NV, NH = NX * NZ, 2 * NY

COLUMNS = (slice(0, 128), slice(128, 384))

F32 = jnp.float32
BF16 = jnp.bfloat16
NT = (((1,), (1,)), ((), ()))
TN = (((0,), (0,)), ((), ()))


def dot(a, b, dims=(((1,), (0,)), ((), ())), precision=None):
    return lax.dot_general(a, b, dims, precision=precision, preferred_element_type=F32)


def low_lanes(shape):
    return lax.broadcasted_iota(jnp.int32, shape, len(shape) - 1) < 64


def head_norm(x):
    low = low_lanes(x.shape)
    sq = x * x
    first = jnp.sum(jnp.where(low, sq, 0.0), axis=-1, keepdims=True)
    second = jnp.sum(jnp.where(low, 0.0, sq), axis=-1, keepdims=True)
    return lax.rsqrt(jnp.where(low, first, second) * (1.0 / 64) + EPS)


def split(x):
    upper = x.astype(BF16)
    return upper, (x - upper.astype(F32)).astype(BF16)


def head_norm_wide(x):
    upper, lower = split(x * x)
    row = lax.broadcasted_iota(jnp.int32, (x.shape[1], x.shape[1]), 0) // 64
    col = lax.broadcasted_iota(jnp.int32, (x.shape[1], x.shape[1]), 1) // 64
    ones = jnp.where(row == col, 1.0, 0.0).astype(BF16)
    return lax.rsqrt((dot(upper, ones) + dot(lower, ones)) * (1.0 / 64) + EPS)


def exact(a, b):
    return dot(a, b, precision=lax.Precision.HIGHEST)


def triple(a, b):
    a_upper, a_lower = split(a)
    b_upper, b_lower = split(b)
    return dot(a_upper, b_upper) + (dot(a_upper, b_lower) + dot(a_lower, b_upper))


def sigmoid(x):
    return 0.5 + 0.5 * jnp.tanh(0.5 * x)


def gray(p):
    return p + (p // 2) * (1 - 2 * (p % 2))


def start_copy(src, dst, send, recv, view, head):
    pltpu.make_async_remote_copy(
        src_ref=src,
        dst_ref=dst,
        send_sem=send,
        recv_sem=recv,
        device_id=(view, head),
        device_id_type=pl.DeviceIdType.MESH,
    ).start()


def wait_bytes(ref, sem):
    pltpu.make_async_copy(ref, ref, sem).wait()


def kernel(
    features,
    attend,
    fast,
    outw,
    mask,
    result,
    stream,
    gathered,
    qkv_w,
    fast_w,
    out_w,
    queries,
    scaled,
    keys,
    values,
    wide,
    total,
    to_sum,
    a_x,
    c_z,
    a_z,
    c_x,
    middle,
    summed,
    attended,
    to_mix,
    mixed,
    w_recv,
    w_send,
    o_recv,
    o_send,
    og_recv,
    og_send,
    g_recv,
    g_send,
    r_recv,
    r_send,
    m_recv,
    m_send,
):
    view, head = lax.axis_index("view"), lax.axis_index("head")
    x, z = view // NZ, view % NZ
    y, core = head // 2, head % 2
    tokens = stream.shape[0]
    length = tokens * NH
    sib = y * 2 + (1 - core)
    right = ((y + 1) % NY) * 2 + core
    left = ((y + NY - 1) % NY) * 2 + core
    opposite = ((y + 2) % NY) * 2 + core
    half = tokens // 2
    pair = tokens * 2

    def aligned(value, to):
        return pl.multiple_of(value, to)

    def normalize(b, part):
        rows = slice(part * half, (part + 1) * half)
        wide_rows = stream[rows, :].astype(F32)
        inv = lax.rsqrt(jnp.mean(wide_rows * wide_rows, axis=-1, keepdims=True) + EPS)
        gathered[b, pl.ds(aligned(head * tokens + part * half, half), half), :] = (
            wide_rows * inv
        ).astype(BF16)

    barrier = pltpu.get_barrier_semaphore()

    def greet(to_view, to_head):
        pl.semaphore_signal(
            barrier, inc=1, device_id=(to_view, to_head), device_id_type=pl.DeviceIdType.MESH
        )

    def greet_z(d, carry):
        greet(x * NZ + (z + d) % NZ, head)
        return carry

    for to in (right, left, sib):
        greet(view, to)
    lax.fori_loop(1, NZ, greet_z, 0)
    for d in range(1, NX):
        greet(((x + d) % NX) * NZ + z, head)
    stream[...] = features[...]
    for b in range(BLOCKS):
        for j in range(3):
            qkv_w[b, pl.ds(aligned(view * 32, 32), 32), j * 128 : (j + 1) * 128] = attend[b, j]
            fast_w[b, j, x, z] = jnp.concatenate([fast[b, 0, j], fast[b, 1, j]], axis=1)
    normalize(0, 0)
    normalize(0, 1)
    pl.semaphore_wait(barrier, 3 + NZ - 1 + NX - 1)

    def tokens_of(b, of_head, part=None):
        if part is None:
            return gathered.at[b, pl.ds(aligned(of_head * tokens, tokens), tokens)]
        return gathered.at[b, pl.ds(aligned(of_head * tokens + part * half, half), half)]

    def send_tokens(b, of_head, part, recv, to, columns=None):
        piece = tokens_of(b, of_head, part)
        if columns is not None:
            piece = piece.at[:, columns]
        start_copy(piece, piece, g_send.at[b], g_recv.at[b, recv], view, to)

    def launch_tokens(b, part):
        send_tokens(b, head, part, part, right)
        send_tokens(b, head, part, 2 + part, left)
        send_tokens(b, head, part, 4, sib)

    def projections_z(b):
        rows = pl.ds(aligned(view * 32, 32), 32)
        for part, columns in enumerate(COLUMNS):
            own = qkv_w.at[b, rows, columns]

            def send(d, carry):
                to = x * NZ + (z + d) % NZ
                start_copy(own, own, w_send.at[b, part], w_recv.at[b, part], to, head)
                return carry

            lax.fori_loop(1, NZ, send, 0)

    def projections_x(b):
        rows = pl.ds(aligned(x * 256, 256), 256)
        for part, columns in enumerate(COLUMNS):
            wait_bytes(qkv_w.at[b, pl.ds(0, 32 * (NZ - 1)), columns], w_recv.at[b, part])
            own = qkv_w.at[b, rows, columns]
            for d in (1, 3, 2):
                to = ((x + d) % NX) * NZ + z
                start_copy(own, own, w_send.at[b, 2 + part], w_recv.at[b, 2 + part], to, head)

    def fast_x(b):
        own = fast_w.at[b, :, x, z]
        for d in (1, 3, 2):
            to = ((x + d) % NX) * NZ + z
            start_copy(own, own, w_send.at[b, 4], w_recv.at[b, 4], to, head)

    def fast_z(b):
        wait_bytes(fast_w.at[b, :, pl.ds(0, NX - 1), 0], w_recv.at[b, 4])
        own = fast_w.at[b, :, :, z]

        def send(d, carry):
            to = x * NZ + (z + d) % NZ
            start_copy(own, own, w_send.at[b, 5], w_recv.at[b, 5], to, head)
            return carry

        lax.fori_loop(1, NZ, send, 0)

    group = view // 4

    def output_fetch(b):
        target = out_w.at[b, pl.ds(aligned(view * 32, 32), 32)]
        target_group = (group - head + NH) % NH

        def send(i, carry):
            to = target_group * 4 + i

            @pl.when(to == view)
            def _():
                pltpu.make_async_copy(outw.at[b], target, o_recv.at[b]).start()

            @pl.when(to != view)
            def _():
                start_copy(outw.at[b], target, o_send.at[b], o_recv.at[b], to, head)

            return carry

        lax.fori_loop(0, 4, send, 0)

    def output_rows(of_head):
        return pl.ds(aligned(((group + of_head) % NH) * 128, 128), 128)

    def output_share(b):
        own = out_w.at[b, output_rows(head)]
        for to in (right, left, opposite):
            start_copy(own, own, og_send.at[b], og_recv.at[b, 0], view, to)
        start_copy(own, own, og_send.at[b], og_recv.at[b, 1], view, sib)

    def output_forward(b):
        wait_bytes(out_w.at[b, pl.ds(0, 3 * 128)], og_recv.at[b, 0])
        for of_head in (right, left, opposite):
            piece = out_w.at[b, output_rows(of_head)]
            start_copy(piece, piece, og_send.at[b], og_recv.at[b, 1], view, sib)

    projections_z(0)
    launch_tokens(0, 0)
    launch_tokens(0, 1)
    fast_x(0)
    projections_x(0)
    fast_z(0)

    def block(b, carry):
        def forward_opposite(part):
            wait_bytes(tokens_of(b, opposite, part).at[:, 0:512], g_recv.at[b, 7 + part])
            wait_bytes(tokens_of(b, opposite, part).at[:, 512:1024], g_recv.at[b, 9 + part])
            send_tokens(b, opposite, part, 11, sib)

        def project(s):
            @pl.when(s == b)
            def _():
                for part in range(2):
                    wait_bytes(tokens_of(b, left, part), g_recv.at[b, part])
                    send_tokens(b, left, part, 7 + part, right, slice(0, 512))
                    wait_bytes(tokens_of(b, right, part), g_recv.at[b, 2 + part])
                    send_tokens(b, right, part, 9 + part, left, slice(512, 1024))
                    send_tokens(b, right, part, 5, sib)
                    send_tokens(b, left, part, 6, sib)

            @pl.when(s == 0)
            def _():
                wait_bytes(tokens_of(b, sib), g_recv.at[b, 4])
                for part, columns in enumerate(COLUMNS):
                    wait_bytes(qkv_w.at[b, pl.ds(0, 256 * (NX - 1)), columns], w_recv.at[b, 2 + part])

            @pl.when(s == 1)
            def _():
                wait_bytes(tokens_of(b, sib), g_recv.at[b, 5])

            @pl.when(s == 2)
            def _():
                wait_bytes(tokens_of(b, sib), g_recv.at[b, 6])

            @pl.when(s == 3)
            def _():
                forward_opposite(1)
                wait_bytes(tokens_of(b, sib), g_recv.at[b, 11])

            rows = pl.ds(aligned(((y + gray(s)) % NY) * pair, pair), pair)
            packed = dot(gathered[b, rows, :], qkv_w[b]).astype(BF16)
            both = packed[:, 0:256].astype(F32)
            both = both * head_norm_wide(both)
            q = both[:, 0:128]
            v = packed[:, 256:384]
            queries[rows, :] = q.astype(BF16)
            scaled[rows, :] = (q * (SCORE_SCALE * math.log2(math.e))).astype(BF16)
            keys[rows, :] = both[:, 128:256].astype(BF16)
            low = low_lanes(v.shape)
            one = jnp.ones_like(v)
            values[0, rows, :] = jnp.where(low, v, one)
            values[1, rows, :] = jnp.where(low, one, v)

        def differentiate(s):
            @pl.when(s == 0)
            def _():
                wait_bytes(fast_w.at[b, :, :, pl.ds(0, NZ - 1)], w_recv.at[b, 5])

                @pl.when(b == 0)
                def _():
                    output_fetch(0)
                    projections_z(1)
                    fast_x(1)

                total[...] = jnp.zeros_like(total)
                for j in range(3):
                    weights = fast_w[b, j].reshape(512, 128)
                    low = low_lanes(weights.shape)
                    wide[j, 0:512, :] = jnp.where(low, weights, jnp.zeros_like(weights))
                    wide[j, 512:1024, :] = jnp.where(low, jnp.zeros_like(weights), weights)

            @pl.when(s == 2)
            def _():
                forward_opposite(0)

            rows = pl.ds(aligned(((y + gray(s)) % NY) * pair, pair), pair)
            k = keys[rows, :]
            low = low_lanes(k.shape)
            zero = jnp.zeros_like(k)
            sign = -mask[:, rows].astype(F32)
            for h in range(2):
                v = values[h, rows, :]
                kh = jnp.where(low, k, zero) if h == 0 else jnp.where(low, zero, k)
                vh = jnp.where(low, v, zero) if h == 0 else jnp.where(low, zero, v)
                f = slice(h * 512, h * 512 + 512)
                first = dot(wide[0, f, :], k, NT)
                third = dot(wide[1, f, :], k, NT)
                back = dot(wide[2, f, :], v, NT) * sign
                sigma = sigmoid(first)
                silu = first * sigma
                hidden = (silu * third * sign).astype(BF16)
                d_third = (back * silu).astype(BF16)
                d_first = (back * third * (sigma + silu * (1.0 - sigma))).astype(BF16)
                total[0] += dot(d_first, kh)
                total[1] += dot(d_third, kh)
                total[2] += dot(hidden, vh)

        def turn(u, carry):
            late = b + (1 - b) * (u // 4)
            s = late * (u // 2) + (1 - late) * (u % 2)
            kind = late * (u % 2) + (1 - late) * (u // 2)

            @pl.when(kind == 0)
            def _():
                project(s)

            @pl.when(kind == 1)
            def _():
                differentiate(s)

            return carry

        lax.fori_loop(0, 2 * NY, turn, 0)

        for j in range(3):
            to_sum[j * 512 : (j + 1) * 512, :] = total[j].astype(BF16)

        def along_x(source, target, sem):
            for d in (1, 3, 2):
                to = (x + d) % NX
                start_copy(
                    source(to), target(d - 1), r_send.at[b, sem], r_recv.at[b, sem], to * NZ + z, head
                )

        def along_z(source, target, sem):
            def send(d, carry):
                to = (z + d) % NZ
                start_copy(
                    source(to), target(d - 1), r_send.at[b, sem], r_recv.at[b, sem], x * NZ + to, head
                )
                return carry

            lax.fori_loop(1, NZ, send, 0)

        def rows_of(ref, start, count):
            return ref.at[pl.ds(aligned(start, 16), count)]

        def add(own, slots):
            return own.astype(F32) + jnp.sum(slots.astype(F32), axis=0)

        along_x(lambda to: rows_of(to_sum, to * 256, 256), lambda i: a_x.at[b, i], 0)
        along_z(lambda to: rows_of(to_sum, 1024 + to * 64, 64), lambda i: c_z.at[b, i], 1)

        def reduce_parts():
            wait_bytes(a_x.at[b], r_recv.at[b, 0])
            own = to_sum[pl.ds(aligned(x * 256, 16), 256), :]
            middle[0:256, :] = add(own, a_x[b]).astype(BF16)
            along_z(lambda to: rows_of(middle, to * 32, 32), lambda i: a_z.at[b, i], 2)
            wait_bytes(c_z.at[b], r_recv.at[b, 1])
            own = to_sum[pl.ds(aligned(1024 + z * 64, 16), 64), :]
            middle[256:320, :] = add(own, c_z[b]).astype(BF16)
            along_x(lambda to: rows_of(middle, 256 + to * 16, 16), lambda i: c_x.at[b, i], 3)

        def spread_parts():
            wait_bytes(a_z.at[b], r_recv.at[b, 2])
            mine = pl.ds(aligned(x * 256 + z * 32, 16), 32)
            own = middle[pl.ds(aligned(z * 32, 16), 32), :]
            summed[b, mine, :] = add(own, a_z[b]).astype(BF16)
            along_z(lambda to: summed.at[b, mine], lambda i: summed.at[b, mine], 4)
            wait_bytes(c_x.at[b], r_recv.at[b, 3])
            last = pl.ds(aligned(1024 + z * 64 + x * 16, 16), 16)
            own = middle[pl.ds(aligned(256 + x * 16, 16), 16), :]
            summed[b, last, :] = add(own, c_x[b]).astype(BF16)
            along_x(lambda to: summed.at[b, last], lambda i: summed.at[b, last], 5)

        def collect_parts():
            wait_bytes(summed.at[b, pl.ds(0, 32 * (NZ - 1))], r_recv.at[b, 4])
            mine = pl.ds(aligned(x * 256, 16), 256)
            along_x(lambda to: summed.at[b, mine], lambda i: summed.at[b, mine], 6)
            wait_bytes(summed.at[b, pl.ds(0, 16 * (NX - 1))], r_recv.at[b, 5])
            last = pl.ds(aligned(1024 + z * 64, 16), 64)
            along_z(lambda to: summed.at[b, last], lambda i: summed.at[b, last], 7)

        def attend_rows(i, carry):
            @pl.when(i == 1)
            def _():
                reduce_parts()
                wait_bytes(out_w.at[b, pl.ds(0, 128)], o_recv.at[b])
                output_share(b)

            rows = pl.ds(aligned(i * 1024, 1024), 1024)
            q = scaled[rows, :]
            low = low_lanes(q.shape)
            zero = jnp.zeros_like(q)
            own = [jnp.where(low, q, zero), jnp.where(low, zero, q)]
            weighted = [jnp.zeros(q.shape, F32)] * 2
            for part in range(length // 256):
                at = slice(part * 256, (part + 1) * 256)
                for h in range(2):
                    expo = jnp.exp2(dot(own[h], keys[at, :], NT)).astype(BF16)
                    weighted[h] = weighted[h] + dot(expo, values[h, at, :])
            out = [each / pltpu.roll(each, 64, 1) for each in weighted]
            attended[rows, :] = jnp.where(low_lanes(out[0].shape), out[0], out[1])
            return carry

        lax.fori_loop(0, length // 1024, attend_rows, 0)
        spread_parts()
        collect_parts()

        wait_bytes(summed.at[b, pl.ds(0, 256 * (NX - 1))], r_recv.at[b, 6])
        wait_bytes(summed.at[b, pl.ds(0, 64 * (NZ - 1))], r_recv.at[b, 7])
        output_forward(b)

        @pl.when(b == 0)
        def _():
            projections_x(1)
            fast_z(1)
            output_fetch(1)

        row = lax.broadcasted_iota(jnp.int32, (128, 128), 0)
        col = lax.broadcasted_iota(jnp.int32, (128, 128), 1)
        same = (row < 64) == (col < 64)
        eye = row == col
        grams, scales = [], []
        for j in range(3):
            gradient = summed[b, j * 512 : (j + 1) * 512, :]
            gram = jnp.where(same, dot(gradient, gradient, TN), 0.0)
            diagonal = jnp.where(eye, gram, 0.0)
            squares = jnp.sum(jnp.where(same, jnp.sum(diagonal, axis=1, keepdims=True), 0.0), axis=0, keepdims=True)
            scale = lax.rsqrt(squares + 1e-06)
            scales.append(scale)
            grams.append(gram * (scale * scale))
        for step in range(NS_STEPS):
            product = exact if step < 2 else triple
            polys = [
                jnp.where(eye, NEWTON[0], 0.0)
                + NEWTON[1] * gram
                + NEWTON[2] * product(gram, gram)
                for gram in grams
            ]
            if step < NS_STEPS - 1:
                halves = [product(poly, gram) for poly, gram in zip(polys, grams)]
                grams = [product(each, poly) for each, poly in zip(halves, polys)]
            if step == 0:
                chains = polys
            else:
                chains = [triple(poly, chain) for poly, chain in zip(polys, chains)]
        for j in range(3):
            gradient = summed[b, j * 512 : (j + 1) * 512, :]
            upper, lower = split(chains[j])
            current = (dot(gradient, upper) + dot(gradient, lower)) * scales[j]
            updated = (fast_w[b, j].reshape(512, 128).astype(F32) - LEARN_RATE * current).astype(BF16)
            low = low_lanes(updated.shape)
            wide[j, 0:512, :] = jnp.where(low, updated, jnp.zeros_like(updated))
            wide[j, 512:1024, :] = jnp.where(low, jnp.zeros_like(updated), updated)

        def apply_rows(u, carry):
            part, s = u // NY, u % NY
            chip = (y + gray(NY - 1 - s)) % NY
            near = pl.ds(aligned((chip * 2 + core) * tokens + part * half, half), half)
            far = pl.ds(aligned((chip * 2 + 1 - core) * tokens + part * half, half), half)
            q = jnp.concatenate([queries[far, :], queries[near, :]], axis=0)
            applied = jnp.zeros(q.shape, F32)
            for block_f in range(2):
                f = slice(block_f * 512, block_f * 512 + 512)
                first = dot(q, wide[0, f, :], NT)
                third = dot(q, wide[1, f, :], NT)
                hidden = (first * sigmoid(first) * third).astype(BF16)
                applied = applied + dot(hidden, wide[2, f, :])
            applied = applied * head_norm(applied)
            to_mix[far, :] = (attended[far, :] + applied[0:half]).astype(BF16)
            to_mix[near, :] = (attended[near, :] + applied[half:]).astype(BF16)
            target = mixed.at[
                b, pl.ds(aligned(part * half, half), half), pl.ds(aligned(head * 128, 128), 128)
            ]
            sems = m_send.at[b], m_recv.at[b, part]
            start_copy(to_mix.at[far], target, *sems, view, chip * 2 + 1 - core)

            @pl.when(s < NY - 1)
            def _():
                start_copy(to_mix.at[near], target, *sems, view, chip * 2 + core)

            @pl.when(s == NY - 1)
            def _():
                target[...] = to_mix[near, :]

            return carry

        lax.fori_loop(0, 2 * NY, apply_rows, 0)

        wait_bytes(out_w.at[b, pl.ds(0, 4 * 128)], og_recv.at[b, 1])
        for part in range(2):
            rows = slice(part * half, (part + 1) * half)
            wait_bytes(mixed.at[b, rows, pl.ds(0, 128 * (NH - 1))], m_recv.at[b, part])
            projected = dot(mixed[b, rows, :], out_w[b])
            stream[rows, :] = (stream[rows, :].astype(F32) + projected).astype(BF16)

            @pl.when(b < BLOCKS - 1)
            def _():
                normalize(b + 1, part)
                launch_tokens(b + 1, part)

        wait_bytes(to_mix.at[pl.ds(0, tokens * (NH - 1))], m_send.at[b])
        for sem, count in enumerate((768, 448, 224, 48, 224, 48, 768, 448)):
            wait_bytes(summed.at[b, pl.ds(0, count)], r_send.at[b, sem])
        wait_bytes(gathered.at[b, pl.ds(0, tokens * 7)], g_send.at[b])
        wait_bytes(out_w.at[b, pl.ds(0, 128 * 7)], og_send.at[b])
        return carry

    lax.fori_loop(0, BLOCKS, block, 0)
    result[...] = stream[...]

    for b in range(BLOCKS):
        for part, columns in enumerate(COLUMNS):
            wait_bytes(qkv_w.at[b, pl.ds(0, 32 * (NZ - 1)), columns], w_send.at[b, part])
            wait_bytes(qkv_w.at[b, pl.ds(0, 256 * (NX - 1)), columns], w_send.at[b, 2 + part])
        wait_bytes(fast_w.at[b, :, pl.ds(0, NX - 1), 0], w_send.at[b, 4])
        wait_bytes(fast_w.at[b, :, :, pl.ds(0, NZ - 1)], w_send.at[b, 5])

    @pl.when(head == 0)
    def _():
        for b in range(BLOCKS):
            wait_bytes(out_w.at[b, pl.ds(0, 96)], o_send.at[b])

    @pl.when(head != 0)
    def _():
        for b in range(BLOCKS):
            wait_bytes(out_w.at[b, pl.ds(0, 128)], o_send.at[b])


def shards(features, attend_weight, output_weight, fast_init, update_mask):
    tokens, width = features.shape
    length = tokens * NH
    vmem = pl.BlockSpec(memory_space=pltpu.VMEM)
    dma = pltpu.SemaphoreType.DMA
    return pl.pallas_call(
        kernel,
        out_shape=jax.ShapeDtypeStruct((tokens, width), BF16),
        in_specs=[vmem] * 5,
        out_specs=vmem,
        scratch_shapes=[
            pltpu.VMEM((tokens, width), BF16),
            pltpu.VMEM((BLOCKS, length, width), BF16),
            pltpu.VMEM((BLOCKS, width, 384), BF16),
            pltpu.VMEM((BLOCKS, 3, NX, NZ, 16, 128), BF16),
            pltpu.VMEM((BLOCKS, width, width), BF16),
            pltpu.VMEM((length, 128), BF16),
            pltpu.VMEM((length, 128), BF16),
            pltpu.VMEM((length, 128), BF16),
            pltpu.VMEM((2, length, 128), BF16),
            pltpu.VMEM((3, 1024, 128), BF16),
            pltpu.VMEM((3, 512, 128), F32),
            pltpu.VMEM((1536, 128), BF16),
            pltpu.VMEM((BLOCKS, NX - 1, 256, 128), BF16),
            pltpu.VMEM((BLOCKS, NZ - 1, 64, 128), BF16),
            pltpu.VMEM((BLOCKS, NZ - 1, 32, 128), BF16),
            pltpu.VMEM((BLOCKS, NX - 1, 16, 128), BF16),
            pltpu.VMEM((320, 128), BF16),
            pltpu.VMEM((BLOCKS, 1536, 128), BF16),
            pltpu.VMEM((length, 128), F32),
            pltpu.VMEM((length, 128), BF16),
            pltpu.VMEM((BLOCKS, tokens, width), BF16),
            dma((BLOCKS, 6)),
            dma((BLOCKS, 6)),
            dma((BLOCKS,)),
            dma((BLOCKS,)),
            dma((BLOCKS, 2)),
            dma((BLOCKS,)),
            dma((BLOCKS, 12)),
            dma((BLOCKS,)),
            dma((BLOCKS, 8)),
            dma((BLOCKS, 8)),
            dma((BLOCKS, 2)),
            dma((BLOCKS,)),
        ],
        compiler_params=pltpu.CompilerParams(
            collective_id=0, has_side_effects=True, vmem_limit_bytes=56 * 1024 * 1024
        ),
        name="lact",
    )(features, attend_weight, jnp.swapaxes(fast_init, 3, 4), output_weight, update_mask)


def solution(mesh):
    return jax.shard_map(
        shards,
        mesh=mesh,
        in_specs=(
            P(("view", "head"), None),
            P(None, None, "view", "head"),
            P(None, "view", None),
            P(None, "head", None, None, "view"),
            P("view", None),
        ),
        out_specs=P(("view", "head"), None),
        check_vma=False,
    )
```

```python
import math

import jax
import jax.numpy as jnp
from jax import lax
from jax.experimental import pallas as pl
from jax.experimental.pallas import tpu as pltpu
from jax.sharding import PartitionSpec as P

BLOCKS = 2
NS_STEPS = 5
NEWTON = (3.4445, -4.775, 2.0315)
LEARN_RATE = 1.0
SCORE_SCALE = 0.25
EPS = 1e-05

NX, NZ, NY = 4, 8, 4
NV, NH = NX * NZ, 2 * NY

COLUMNS = (slice(0, 128), slice(128, 384))

F32 = jnp.float32
BF16 = jnp.bfloat16
NT = (((1,), (1,)), ((), ()))
TN = (((0,), (0,)), ((), ()))


def dot(a, b, dims=(((1,), (0,)), ((), ())), precision=None):
    return lax.dot_general(a, b, dims, precision=precision, preferred_element_type=F32)


def low_lanes(shape):
    return lax.broadcasted_iota(jnp.int32, shape, len(shape) - 1) < 64


def head_norm(x):
    low = low_lanes(x.shape)
    sq = x * x
    first = jnp.sum(jnp.where(low, sq, 0.0), axis=-1, keepdims=True)
    second = jnp.sum(jnp.where(low, 0.0, sq), axis=-1, keepdims=True)
    return lax.rsqrt(jnp.where(low, first, second) * (1.0 / 64) + EPS)


def split(x):
    upper = x.astype(BF16)
    return upper, (x - upper.astype(F32)).astype(BF16)


def head_norm_wide(x):
    upper, lower = split(x * x)
    row = lax.broadcasted_iota(jnp.int32, (x.shape[1], x.shape[1]), 0) // 64
    col = lax.broadcasted_iota(jnp.int32, (x.shape[1], x.shape[1]), 1) // 64
    ones = jnp.where(row == col, 1.0, 0.0).astype(BF16)
    return lax.rsqrt((dot(upper, ones) + dot(lower, ones)) * (1.0 / 64) + EPS)


def exact(a, b):
    return dot(a, b, precision=lax.Precision.HIGHEST)


def triple(a, b):
    a_upper, a_lower = split(a)
    b_upper, b_lower = split(b)
    return dot(a_upper, b_upper) + (dot(a_upper, b_lower) + dot(a_lower, b_upper))


def sigmoid(x):
    return 0.5 + 0.5 * jnp.tanh(0.5 * x)


def gray(p):
    return p + (p // 2) * (1 - 2 * (p % 2))


def start_copy(src, dst, send, recv, view, head):
    pltpu.make_async_remote_copy(
        src_ref=src,
        dst_ref=dst,
        send_sem=send,
        recv_sem=recv,
        device_id=(view, head),
        device_id_type=pl.DeviceIdType.MESH,
    ).start()


def wait_bytes(ref, sem):
    pltpu.make_async_copy(ref, ref, sem).wait()


def kernel(
    features,
    attend,
    fast,
    outw,
    mask,
    result,
    stream,
    gathered,
    qkv_w,
    fast_w,
    out_w,
    queries,
    scaled,
    keys,
    values,
    wide,
    total,
    to_sum,
    a_x,
    c_z,
    a_z,
    c_x,
    middle,
    summed,
    attended,
    to_mix,
    mixed,
    w_recv,
    w_send,
    o_recv,
    o_send,
    og_recv,
    og_send,
    g_recv,
    g_send,
    r_recv,
    r_send,
    m_recv,
    m_send,
):
    view, head = lax.axis_index("view"), lax.axis_index("head")
    x, z = view // NZ, view % NZ
    y, core = head // 2, head % 2
    tokens = stream.shape[0]
    length = tokens * NH
    sib = y * 2 + (1 - core)
    right = ((y + 1) % NY) * 2 + core
    left = ((y + NY - 1) % NY) * 2 + core
    opposite = ((y + 2) % NY) * 2 + core
    half = tokens // 2
    pair = tokens * 2

    def aligned(value, to):
        return pl.multiple_of(value, to)

    def normalize(b, part):
        rows = slice(part * half, (part + 1) * half)
        wide_rows = stream[rows, :].astype(F32)
        inv = lax.rsqrt(jnp.mean(wide_rows * wide_rows, axis=-1, keepdims=True) + EPS)
        gathered[b, pl.ds(aligned(head * tokens + part * half, half), half), :] = (
            wide_rows * inv
        ).astype(BF16)

    barrier = pltpu.get_barrier_semaphore()

    def greet(to_view, to_head):
        pl.semaphore_signal(
            barrier, inc=1, device_id=(to_view, to_head), device_id_type=pl.DeviceIdType.MESH
        )

    def greet_z(d, carry):
        greet(x * NZ + (z + d) % NZ, head)
        return carry

    for to in (right, left, sib):
        greet(view, to)
    lax.fori_loop(1, NZ, greet_z, 0)
    for d in range(1, NX):
        greet(((x + d) % NX) * NZ + z, head)
    stream[...] = features[...]
    for b in range(BLOCKS):
        for j in range(3):
            qkv_w[b, pl.ds(aligned(view * 32, 32), 32), j * 128 : (j + 1) * 128] = attend[b, j]
            fast_w[b, j, x, z] = jnp.concatenate([fast[b, 0, j], fast[b, 1, j]], axis=1)
    normalize(0, 0)
    normalize(0, 1)
    pl.semaphore_wait(barrier, 3 + NZ - 1 + NX - 1)

    def tokens_of(b, of_head, part=None):
        if part is None:
            return gathered.at[b, pl.ds(aligned(of_head * tokens, tokens), tokens)]
        return gathered.at[b, pl.ds(aligned(of_head * tokens + part * half, half), half)]

    def send_tokens(b, of_head, part, recv, to, columns=None):
        piece = tokens_of(b, of_head, part)
        if columns is not None:
            piece = piece.at[:, columns]
        start_copy(piece, piece, g_send.at[b], g_recv.at[b, recv], view, to)

    def launch_tokens(b, part):
        send_tokens(b, head, part, part, right)
        send_tokens(b, head, part, 2 + part, left)
        send_tokens(b, head, part, 4, sib)

    def projections_z(b):
        rows = pl.ds(aligned(view * 32, 32), 32)
        for part, columns in enumerate(COLUMNS):
            own = qkv_w.at[b, rows, columns]

            def send(d, carry):
                to = x * NZ + (z + d) % NZ
                start_copy(own, own, w_send.at[b, part], w_recv.at[b, part], to, head)
                return carry

            lax.fori_loop(1, NZ, send, 0)

    def projections_x(b):
        rows = pl.ds(aligned(x * 256, 256), 256)
        for part, columns in enumerate(COLUMNS):
            wait_bytes(qkv_w.at[b, pl.ds(0, 32 * (NZ - 1)), columns], w_recv.at[b, part])
            own = qkv_w.at[b, rows, columns]
            for d in (1, 3, 2):
                to = ((x + d) % NX) * NZ + z
                start_copy(own, own, w_send.at[b, 2 + part], w_recv.at[b, 2 + part], to, head)

    def fast_x(b):
        own = fast_w.at[b, :, x, z]
        for d in (1, 3, 2):
            to = ((x + d) % NX) * NZ + z
            start_copy(own, own, w_send.at[b, 4], w_recv.at[b, 4], to, head)

    def fast_z(b):
        wait_bytes(fast_w.at[b, :, pl.ds(0, NX - 1), 0], w_recv.at[b, 4])
        own = fast_w.at[b, :, :, z]

        def send(d, carry):
            to = x * NZ + (z + d) % NZ
            start_copy(own, own, w_send.at[b, 5], w_recv.at[b, 5], to, head)
            return carry

        lax.fori_loop(1, NZ, send, 0)

    group = view // 4

    def output_fetch(b):
        target = out_w.at[b, pl.ds(aligned(view * 32, 32), 32)]
        target_group = (group - head + NH) % NH

        def send(i, carry):
            to = target_group * 4 + i

            @pl.when(to == view)
            def _():
                pltpu.make_async_copy(outw.at[b], target, o_recv.at[b]).start()

            @pl.when(to != view)
            def _():
                start_copy(outw.at[b], target, o_send.at[b], o_recv.at[b], to, head)

            return carry

        lax.fori_loop(0, 4, send, 0)

    def output_rows(of_head):
        return pl.ds(aligned(((group + of_head) % NH) * 128, 128), 128)

    def output_share(b):
        own = out_w.at[b, output_rows(head)]
        for to in (right, left, opposite):
            start_copy(own, own, og_send.at[b], og_recv.at[b, 0], view, to)
        start_copy(own, own, og_send.at[b], og_recv.at[b, 1], view, sib)

    def output_forward(b):
        wait_bytes(out_w.at[b, pl.ds(0, 3 * 128)], og_recv.at[b, 0])
        for of_head in (right, left, opposite):
            piece = out_w.at[b, output_rows(of_head)]
            start_copy(piece, piece, og_send.at[b], og_recv.at[b, 1], view, sib)

    projections_z(0)
    launch_tokens(0, 0)
    launch_tokens(0, 1)
    fast_x(0)
    projections_x(0)
    fast_z(0)

    def block(b, carry):
        def forward_opposite(part):
            wait_bytes(tokens_of(b, opposite, part).at[:, 0:512], g_recv.at[b, 7 + part])
            wait_bytes(tokens_of(b, opposite, part).at[:, 512:1024], g_recv.at[b, 9 + part])
            send_tokens(b, opposite, part, 11, sib)

        def project(s):
            @pl.when(s == b)
            def _():
                for part in range(2):
                    wait_bytes(tokens_of(b, left, part), g_recv.at[b, part])
                    send_tokens(b, left, part, 7 + part, right, slice(0, 512))
                    wait_bytes(tokens_of(b, right, part), g_recv.at[b, 2 + part])
                    send_tokens(b, right, part, 9 + part, left, slice(512, 1024))
                    send_tokens(b, right, part, 5, sib)
                    send_tokens(b, left, part, 6, sib)

            @pl.when(s == 0)
            def _():
                wait_bytes(tokens_of(b, sib), g_recv.at[b, 4])
                for part, columns in enumerate(COLUMNS):
                    wait_bytes(qkv_w.at[b, pl.ds(0, 256 * (NX - 1)), columns], w_recv.at[b, 2 + part])

            @pl.when(s == 1)
            def _():
                wait_bytes(tokens_of(b, sib), g_recv.at[b, 5])

            @pl.when(s == 2)
            def _():
                wait_bytes(tokens_of(b, sib), g_recv.at[b, 6])

            @pl.when(s == 3)
            def _():
                forward_opposite(1)
                wait_bytes(tokens_of(b, sib), g_recv.at[b, 11])

            rows = pl.ds(aligned(((y + gray(s)) % NY) * pair, pair), pair)
            packed = dot(gathered[b, rows, :], qkv_w[b]).astype(BF16)
            both = packed[:, 0:256].astype(F32)
            both = both * head_norm_wide(both)
            q = both[:, 0:128]
            v = packed[:, 256:384]
            queries[rows, :] = q.astype(BF16)
            scaled[rows, :] = (q * (SCORE_SCALE * math.log2(math.e))).astype(BF16)
            keys[rows, :] = both[:, 128:256].astype(BF16)
            low = low_lanes(v.shape)
            one = jnp.ones_like(v)
            values[0, rows, :] = jnp.where(low, v, one)
            values[1, rows, :] = jnp.where(low, one, v)

        def differentiate(s):
            @pl.when(s == 0)
            def _():
                wait_bytes(fast_w.at[b, :, :, pl.ds(0, NZ - 1)], w_recv.at[b, 5])

                @pl.when(b == 0)
                def _():
                    output_fetch(0)
                    projections_z(1)
                    fast_x(1)

                total[...] = jnp.zeros_like(total)
                for j in range(3):
                    weights = fast_w[b, j].reshape(512, 128)
                    low = low_lanes(weights.shape)
                    wide[j, 0:512, :] = jnp.where(low, weights, jnp.zeros_like(weights))
                    wide[j, 512:1024, :] = jnp.where(low, jnp.zeros_like(weights), weights)

            @pl.when(s == 2)
            def _():
                forward_opposite(0)

            rows = pl.ds(aligned(((y + gray(s)) % NY) * pair, pair), pair)
            k = keys[rows, :]
            low = low_lanes(k.shape)
            zero = jnp.zeros_like(k)
            sign = -mask[:, rows].astype(F32)
            for h in range(2):
                v = values[h, rows, :]
                kh = jnp.where(low, k, zero) if h == 0 else jnp.where(low, zero, k)
                vh = jnp.where(low, v, zero) if h == 0 else jnp.where(low, zero, v)
                f = slice(h * 512, h * 512 + 512)
                first = dot(wide[0, f, :], k, NT)
                third = dot(wide[1, f, :], k, NT)
                back = dot(wide[2, f, :], v, NT) * sign
                sigma = sigmoid(first)
                silu = first * sigma
                hidden = (silu * third * sign).astype(BF16)
                d_third = (back * silu).astype(BF16)
                d_first = (back * third * (sigma + silu * (1.0 - sigma))).astype(BF16)
                total[0] += dot(d_first, kh)
                total[1] += dot(d_third, kh)
                total[2] += dot(hidden, vh)

        def turn(u, carry):
            late = b + (1 - b) * (u // 4)
            s = late * (u // 2) + (1 - late) * (u % 2)
            kind = late * (u % 2) + (1 - late) * (u // 2)

            @pl.when(kind == 0)
            def _():
                project(s)

            @pl.when(kind == 1)
            def _():
                differentiate(s)

            return carry

        lax.fori_loop(0, 2 * NY, turn, 0)

        for j in range(3):
            to_sum[j * 512 : (j + 1) * 512, :] = total[j].astype(BF16)

        def along_x(source, target, sem):
            for d in (1, 3, 2):
                to = (x + d) % NX
                start_copy(
                    source(to), target(d - 1), r_send.at[b, sem], r_recv.at[b, sem], to * NZ + z, head
                )

        def along_z(source, target, sem):
            def send(d, carry):
                to = (z + d) % NZ
                start_copy(
                    source(to), target(d - 1), r_send.at[b, sem], r_recv.at[b, sem], x * NZ + to, head
                )
                return carry

            lax.fori_loop(1, NZ, send, 0)

        def rows_of(ref, start, count):
            return ref.at[pl.ds(aligned(start, 16), count)]

        def add(own, slots):
            return own.astype(F32) + jnp.sum(slots.astype(F32), axis=0)

        along_x(lambda to: rows_of(to_sum, to * 256, 256), lambda i: a_x.at[b, i], 0)
        along_z(lambda to: rows_of(to_sum, 1024 + to * 64, 64), lambda i: c_z.at[b, i], 1)

        def reduce_parts():
            wait_bytes(a_x.at[b], r_recv.at[b, 0])
            own = to_sum[pl.ds(aligned(x * 256, 16), 256), :]
            middle[0:256, :] = add(own, a_x[b]).astype(BF16)
            along_z(lambda to: rows_of(middle, to * 32, 32), lambda i: a_z.at[b, i], 2)
            wait_bytes(c_z.at[b], r_recv.at[b, 1])
            own = to_sum[pl.ds(aligned(1024 + z * 64, 16), 64), :]
            middle[256:320, :] = add(own, c_z[b]).astype(BF16)
            along_x(lambda to: rows_of(middle, 256 + to * 16, 16), lambda i: c_x.at[b, i], 3)

        def spread_parts():
            wait_bytes(a_z.at[b], r_recv.at[b, 2])
            mine = pl.ds(aligned(x * 256 + z * 32, 16), 32)
            own = middle[pl.ds(aligned(z * 32, 16), 32), :]
            summed[b, mine, :] = add(own, a_z[b]).astype(BF16)
            along_z(lambda to: summed.at[b, mine], lambda i: summed.at[b, mine], 4)
            wait_bytes(c_x.at[b], r_recv.at[b, 3])
            last = pl.ds(aligned(1024 + z * 64 + x * 16, 16), 16)
            own = middle[pl.ds(aligned(256 + x * 16, 16), 16), :]
            summed[b, last, :] = add(own, c_x[b]).astype(BF16)
            along_x(lambda to: summed.at[b, last], lambda i: summed.at[b, last], 5)

        def collect_parts():
            wait_bytes(summed.at[b, pl.ds(0, 32 * (NZ - 1))], r_recv.at[b, 4])
            mine = pl.ds(aligned(x * 256, 16), 256)
            along_x(lambda to: summed.at[b, mine], lambda i: summed.at[b, mine], 6)
            wait_bytes(summed.at[b, pl.ds(0, 16 * (NX - 1))], r_recv.at[b, 5])
            last = pl.ds(aligned(1024 + z * 64, 16), 64)
            along_z(lambda to: summed.at[b, last], lambda i: summed.at[b, last], 7)

        def attend_rows(i, carry):
            @pl.when(i == 1)
            def _():
                reduce_parts()
                wait_bytes(out_w.at[b, pl.ds(0, 128)], o_recv.at[b])
                output_share(b)

            rows = pl.ds(aligned(i * 1024, 1024), 1024)
            q = scaled[rows, :]
            low = low_lanes(q.shape)
            zero = jnp.zeros_like(q)
            own = [jnp.where(low, q, zero), jnp.where(low, zero, q)]
            weighted = [jnp.zeros(q.shape, F32)] * 2
            for part in range(length // 256):
                at = slice(part * 256, (part + 1) * 256)
                for h in range(2):
                    expo = jnp.exp2(dot(own[h], keys[at, :], NT)).astype(BF16)
                    weighted[h] = weighted[h] + dot(expo, values[h, at, :])
            out = [each / pltpu.roll(each, 64, 1) for each in weighted]
            attended[rows, :] = jnp.where(low_lanes(out[0].shape), out[0], out[1])
            return carry

        lax.fori_loop(0, length // 1024, attend_rows, 0)
        spread_parts()
        collect_parts()

        wait_bytes(summed.at[b, pl.ds(0, 256 * (NX - 1))], r_recv.at[b, 6])
        wait_bytes(summed.at[b, pl.ds(0, 64 * (NZ - 1))], r_recv.at[b, 7])
        output_forward(b)

        @pl.when(b == 0)
        def _():
            projections_x(1)
            fast_z(1)
            output_fetch(1)

        row = lax.broadcasted_iota(jnp.int32, (128, 128), 0)
        col = lax.broadcasted_iota(jnp.int32, (128, 128), 1)
        same = (row < 64) == (col < 64)
        eye = row == col
        grams, scales = [], []
        for j in range(3):
            gradient = summed[b, j * 512 : (j + 1) * 512, :]
            gram = jnp.where(same, dot(gradient, gradient, TN), 0.0)
            diagonal = jnp.where(eye, gram, 0.0)
            squares = jnp.sum(jnp.where(same, jnp.sum(diagonal, axis=1, keepdims=True), 0.0), axis=0, keepdims=True)
            scale = lax.rsqrt(squares + 1e-06)
            scales.append(scale)
            grams.append(gram * (scale * scale))
        for step in range(NS_STEPS):
            product = exact if step < 1 else triple
            polys = [
                jnp.where(eye, NEWTON[0], 0.0)
                + NEWTON[1] * gram
                + NEWTON[2] * product(gram, gram)
                for gram in grams
            ]
            if step < NS_STEPS - 1:
                halves = [product(poly, gram) for poly, gram in zip(polys, grams)]
                grams = [product(each, poly) for each, poly in zip(halves, polys)]
            if step == 0:
                chains = polys
            else:
                chains = [triple(poly, chain) for poly, chain in zip(polys, chains)]
        for j in range(3):
            gradient = summed[b, j * 512 : (j + 1) * 512, :]
            upper, lower = split(chains[j])
            current = (dot(gradient, upper) + dot(gradient, lower)) * scales[j]
            updated = (fast_w[b, j].reshape(512, 128).astype(F32) - LEARN_RATE * current).astype(BF16)
            low = low_lanes(updated.shape)
            wide[j, 0:512, :] = jnp.where(low, updated, jnp.zeros_like(updated))
            wide[j, 512:1024, :] = jnp.where(low, jnp.zeros_like(updated), updated)

        def apply_rows(u, carry):
            part, s = u // NY, u % NY
            chip = (y + gray(NY - 1 - s)) % NY
            near = pl.ds(aligned((chip * 2 + core) * tokens + part * half, half), half)
            far = pl.ds(aligned((chip * 2 + 1 - core) * tokens + part * half, half), half)
            q = jnp.concatenate([queries[far, :], queries[near, :]], axis=0)
            applied = jnp.zeros(q.shape, F32)
            for block_f in range(2):
                f = slice(block_f * 512, block_f * 512 + 512)
                first = dot(q, wide[0, f, :], NT)
                third = dot(q, wide[1, f, :], NT)
                hidden = (first * sigmoid(first) * third).astype(BF16)
                applied = applied + dot(hidden, wide[2, f, :])
            applied = applied * head_norm(applied)
            to_mix[far, :] = (attended[far, :] + applied[0:half]).astype(BF16)
            to_mix[near, :] = (attended[near, :] + applied[half:]).astype(BF16)
            target = mixed.at[
                b, pl.ds(aligned(part * half, half), half), pl.ds(aligned(head * 128, 128), 128)
            ]
            sems = m_send.at[b], m_recv.at[b, part]
            start_copy(to_mix.at[far], target, *sems, view, chip * 2 + 1 - core)

            @pl.when(s < NY - 1)
            def _():
                start_copy(to_mix.at[near], target, *sems, view, chip * 2 + core)

            @pl.when(s == NY - 1)
            def _():
                target[...] = to_mix[near, :]

            return carry

        lax.fori_loop(0, 2 * NY, apply_rows, 0)

        wait_bytes(out_w.at[b, pl.ds(0, 4 * 128)], og_recv.at[b, 1])
        for part in range(2):
            rows = slice(part * half, (part + 1) * half)
            wait_bytes(mixed.at[b, rows, pl.ds(0, 128 * (NH - 1))], m_recv.at[b, part])
            projected = dot(mixed[b, rows, :], out_w[b])
            stream[rows, :] = (stream[rows, :].astype(F32) + projected).astype(BF16)

            @pl.when(b < BLOCKS - 1)
            def _():
                normalize(b + 1, part)
                launch_tokens(b + 1, part)

        wait_bytes(to_mix.at[pl.ds(0, tokens * (NH - 1))], m_send.at[b])
        for sem, count in enumerate((768, 448, 224, 48, 224, 48, 768, 448)):
            wait_bytes(summed.at[b, pl.ds(0, count)], r_send.at[b, sem])
        wait_bytes(gathered.at[b, pl.ds(0, tokens * 7)], g_send.at[b])
        wait_bytes(out_w.at[b, pl.ds(0, 128 * 7)], og_send.at[b])
        return carry

    lax.fori_loop(0, BLOCKS, block, 0)
    result[...] = stream[...]

    for b in range(BLOCKS):
        for part, columns in enumerate(COLUMNS):
            wait_bytes(qkv_w.at[b, pl.ds(0, 32 * (NZ - 1)), columns], w_send.at[b, part])
            wait_bytes(qkv_w.at[b, pl.ds(0, 256 * (NX - 1)), columns], w_send.at[b, 2 + part])
        wait_bytes(fast_w.at[b, :, pl.ds(0, NX - 1), 0], w_send.at[b, 4])
        wait_bytes(fast_w.at[b, :, :, pl.ds(0, NZ - 1)], w_send.at[b, 5])

    @pl.when(head == 0)
    def _():
        for b in range(BLOCKS):
            wait_bytes(out_w.at[b, pl.ds(0, 96)], o_send.at[b])

    @pl.when(head != 0)
    def _():
        for b in range(BLOCKS):
            wait_bytes(out_w.at[b, pl.ds(0, 128)], o_send.at[b])


def shards(features, attend_weight, output_weight, fast_init, update_mask):
    tokens, width = features.shape
    length = tokens * NH
    vmem = pl.BlockSpec(memory_space=pltpu.VMEM)
    dma = pltpu.SemaphoreType.DMA
    return pl.pallas_call(
        kernel,
        out_shape=jax.ShapeDtypeStruct((tokens, width), BF16),
        in_specs=[vmem] * 5,
        out_specs=vmem,
        scratch_shapes=[
            pltpu.VMEM((tokens, width), BF16),
            pltpu.VMEM((BLOCKS, length, width), BF16),
            pltpu.VMEM((BLOCKS, width, 384), BF16),
            pltpu.VMEM((BLOCKS, 3, NX, NZ, 16, 128), BF16),
            pltpu.VMEM((BLOCKS, width, width), BF16),
            pltpu.VMEM((length, 128), BF16),
            pltpu.VMEM((length, 128), BF16),
            pltpu.VMEM((length, 128), BF16),
            pltpu.VMEM((2, length, 128), BF16),
            pltpu.VMEM((3, 1024, 128), BF16),
            pltpu.VMEM((3, 512, 128), F32),
            pltpu.VMEM((1536, 128), BF16),
            pltpu.VMEM((BLOCKS, NX - 1, 256, 128), BF16),
            pltpu.VMEM((BLOCKS, NZ - 1, 64, 128), BF16),
            pltpu.VMEM((BLOCKS, NZ - 1, 32, 128), BF16),
            pltpu.VMEM((BLOCKS, NX - 1, 16, 128), BF16),
            pltpu.VMEM((320, 128), BF16),
            pltpu.VMEM((BLOCKS, 1536, 128), BF16),
            pltpu.VMEM((length, 128), F32),
            pltpu.VMEM((length, 128), BF16),
            pltpu.VMEM((BLOCKS, tokens, width), BF16),
            dma((BLOCKS, 6)),
            dma((BLOCKS, 6)),
            dma((BLOCKS,)),
            dma((BLOCKS,)),
            dma((BLOCKS, 2)),
            dma((BLOCKS,)),
            dma((BLOCKS, 12)),
            dma((BLOCKS,)),
            dma((BLOCKS, 8)),
            dma((BLOCKS, 8)),
            dma((BLOCKS, 2)),
            dma((BLOCKS,)),
        ],
        compiler_params=pltpu.CompilerParams(
            collective_id=0, has_side_effects=True, vmem_limit_bytes=56 * 1024 * 1024
        ),
        name="lact",
    )(features, attend_weight, jnp.swapaxes(fast_init, 3, 4), output_weight, update_mask)


def solution(mesh):
    return jax.shard_map(
        shards,
        mesh=mesh,
        in_specs=(
            P(("view", "head"), None),
            P(None, None, "view", "head"),
            P(None, "view", None),
            P(None, "head", None, None, "view"),
            P("view", None),
        ),
        out_specs=P(("view", "head"), None),
        check_vma=False,
    )
```
